256 devices in a mesh: dp: 16 (over x, y_hi, core), vocab: 8 (over z), tensor: 2 (over y_lo).
Axes of the slice: x: 4, y: 4 (y_hi: 2, y_lo: 2; y = y_hi * 2 + y_lo), z: 8, core: 2. Of those that a mesh axis runs over, the one named last changes fastest.
Arguments:
- residual: bfloat16 [1408, 4096], P('dp', 'tensor'), may hold values from -400 to 400
- norm_gain: float32 [4096], P('tensor'), may hold values from 0.1 to 1.9
- gain_dir: float32 [4096], P('tensor'), may hold values from -6 to 6
- head_weight: bfloat16 [4096, 81920], P('tensor', ('dp', 'vocab')), may hold values from -0.8 to 0.8
- head_dir: bfloat16 [4096, 81920], P('tensor', ('dp', 'vocab')), may hold values from -0.25 to 0.25
- sampled: int32 [1408], replicated, may hold values from 0 to 81919
Outputs:
- fisher_head: float32 [4096, 81920], P('tensor', ('dp', 'vocab'))
- fisher_gain: float32 [4096], P('tensor')
The draws below stay inside these ranges and needn't reach their ends.
All inputs are finite; a program needn't handle non-finite values.
Results may differ from the reference program's by a relative error of at most 0.012.
The reference program's roundings to bfloat16 on the way (of `normed`, `hidden`, `tangent` and `cotangent`) count: a program that leaves them out, or rounds other values in their place, can miss the bound.
Values may be sent and summed in bfloat16 or wider, within the bound.
No kernel may reach another device: no remote copies, remote signals or barrier semaphores. Data moves between devices by JAX's collectives and lax.ppermute only.
A program may use at most 128 MiB of HBM per device.

```python
import math
import jax
import jax.numpy as jnp
import numpy as np
from jax import lax

D = 4096
TOKENS = 1408
VOCAB = 81920


def draw_residual(key, part):
    key = jax.random.fold_in(key, 3)
    noise_key, row_key, col_key = jax.random.split(key, 3)
    row_scale = jnp.exp(jax.random.uniform(row_key, (TOKENS, 1), jnp.float32) * math.log(10.0))
    col_scale = jnp.exp(jax.random.uniform(col_key, (1, D), jnp.float32) * math.log(10.0))
    noise = jnp.clip(jax.random.normal(noise_key, (TOKENS, D), jnp.float32), -4.0, 4.0)
    entries = noise * row_scale * col_scale
    return entries.astype(jnp.bfloat16)


def draw_head_weight(key, part):
    key = jax.random.fold_in(key, 5)
    noise_key, col_key = jax.random.split(key)
    ramp = 1.0 + 2.0 * jnp.arange(VOCAB).astype(jnp.float32) / VOCAB
    col_scale = jnp.exp(jax.random.uniform(col_key, (1, VOCAB), jnp.float32) * math.log(10.0)) * 0.4 * ramp[None, :] / math.sqrt(D)
    noise = jnp.clip(jax.random.normal(noise_key, (D, VOCAB), jnp.float32), -4.0, 4.0)
    entries = noise * col_scale
    return entries.astype(jnp.bfloat16)


def set_ends(values, key, least, top_value):
    longest = values.shape.index(max(values.shape))
    spots = []
    for shift in (0, 1):
        where = [jax.random.randint(jax.random.fold_in(key, axis), (), 0, length) for axis, length in enumerate(values.shape)]
        where[longest] = (where[longest] + shift) % values.shape[longest]
        spots.append(tuple(where))
    return values.at[spots[0]].set(least).at[spots[1]].set(top_value)


def shard_levels(key, extent, pieces, low, high):
    gain = 1.0
    for position, shards_of in pieces:
        draws = jax.random.uniform(jax.random.fold_in(jax.random.fold_in(key, 6), position), (shards_of,), jnp.float32, low / len(pieces), high / len(pieces))
        gain = gain * jnp.repeat(jnp.exp(draws), extent[position] // shards_of).reshape((-1,) + (1,) * (len(extent) - 1 - position))
    return gain


def skewed_wide(own_key, extent, amount, skew):
    portions = [min(1 << octave, amount + 1 - (1 << octave)) * (1 << 20) // math.isqrt((1 << octave) ** skew) + 1 for octave in range((amount + 1).bit_length()) if 1 << octave <= amount]
    deviation = 1 + sum(portions) // (1 << 30)
    listing = np.cumsum(np.array([max(1, weight // deviation) for weight in portions]))
    ticket = jax.random.randint(jax.random.fold_in(own_key, 1), extent, 0, int(listing[len(portions) - 1]))
    start = jnp.left_shift(1, jnp.searchsorted(jnp.asarray(listing, jnp.int32), ticket, side="right").astype(jnp.int32))
    rank = start - 1 + jax.random.randint(jax.random.fold_in(own_key, 4), extent, 0, 1 << 30) % jnp.minimum(start, amount + 1 - start)
    return jax.random.permutation(jax.random.fold_in(own_key, 2), amount)[rank].astype(jnp.int32)


def normal_values(rng, dims, width, most, cuts=(), kind=jnp.bfloat16):
    result = width * jax.random.normal(rng, dims, jnp.float32)
    if cuts:
        result = result * shard_levels(rng, dims, cuts, -0.22, 0.18)
    return jnp.clip(result, -most, most).astype(kind)


def setup_inputs(seed: int = 0) -> dict:
    keys = jax.random.split(jax.random.key(seed), 7)
    return {
        "residual": draw_residual(jax.random.fold_in(keys[6], 71), 0),
        "norm_gain": jnp.clip(1.0 + 0.18 * jax.random.normal(keys[1], (D,), jnp.float32), 0.1, 1.9),
        "gain_dir": normal_values(keys[2], (D,), 1.0, 6.0, ((0, 2),), jnp.float32),
        "head_weight": draw_head_weight(jax.random.fold_in(keys[6], 71), 0),
        "head_dir": normal_values(keys[4], (D, VOCAB), (D // 9) ** -0.5, 0.25, ((0, 2), (1, 128))),
        "sampled": set_ends(skewed_wide(keys[5], (TOKENS,), VOCAB, 2), jax.random.fold_in(keys[5], 3), 0, VOCAB - 1).astype(jnp.int32),
    }


EPSILON = 1e-06

def reference(residual, norm_gain, gain_dir, head_weight, head_dir, sampled):
    entries = residual.astype(jnp.float32)
    inverse = lax.rsqrt(lax.optimization_barrier(jnp.mean(entries * entries, axis=1, keepdims=True)) + EPSILON)
    normed = (entries * inverse).astype(jnp.bfloat16)
    spread = normed.astype(jnp.float32)
    hidden = (spread * norm_gain).astype(jnp.bfloat16)
    tangent = (spread * gain_dir).astype(jnp.bfloat16)
    logits = jnp.dot(hidden, head_weight, preferred_element_type=jnp.float32)
    tangent_logits = jnp.dot(hidden, head_dir, preferred_element_type=jnp.float32) + jnp.dot(tangent, head_weight, preferred_element_type=jnp.float32)
    row_top = lax.optimization_barrier(jnp.max(logits, axis=1, keepdims=True))
    scaled_exp = jnp.exp(logits - row_top)
    row_total = lax.optimization_barrier(jnp.sum(scaled_exp, axis=1, keepdims=True))
    row_probs = scaled_exp / row_total
    weighted = lax.optimization_barrier(jnp.sum(scaled_exp * tangent_logits, axis=1, keepdims=True)) / row_total
    picked = jnp.take_along_axis(tangent_logits, sampled[:, None].astype(jnp.int32), axis=1)
    is_picked = (jnp.arange(logits.shape[1], dtype=jnp.int32)[None, :] == sampled[:, None].astype(jnp.int32)).astype(jnp.float32)
    cotangent = ((picked - weighted) * (is_picked - row_probs)).astype(jnp.bfloat16)
    product = lax.dot_general(normed, cotangent, (((0,), (0,)), ((), ())), preferred_element_type=jnp.float32)
    fisher_head = norm_gain[:, None] * product
    fisher_gain = lax.optimization_barrier(jnp.sum(head_weight.astype(jnp.float32) * product, axis=1))
    return (fisher_head, fisher_gain)
```

```python
import jax
import jax.numpy as jnp
from jax import lax
from jax.sharding import PartitionSpec as P

EPSILON = 1e-06


def everyone(x, axis):
    count = lax.axis_size(axis)
    copies = jnp.broadcast_to(x[None], (count,) + x.shape)
    return lax.all_to_all(copies, axis, 0, 0, tiled=True)


def small_sum(x, axes):
    for axis in axes:
        x = jnp.sum(everyone(x, axis), axis=0)
    return x


def merge_stats(stats, axes):
    for axis in axes:
        parts = everyone(stats, axis)
        top = jnp.max(parts[:, 0], axis=0)
        factor = jnp.exp(parts[:, 0] - top[None])
        total = jnp.sum(factor * parts[:, 1], axis=0)
        weighted = jnp.sum(factor * parts[:, 2], axis=0)
        picked = jnp.sum(parts[:, 3], axis=0)
        stats = jnp.stack([top, total, weighted, picked])
    return stats


def local(residual, norm_gain, gain_dir, head_weight, head_dir, sampled):
    full_width = residual.shape[1] * lax.axis_size("tensor")
    entries = residual.astype(jnp.float32)
    squares = lax.psum(jnp.sum(entries * entries, axis=1), "tensor")
    normed = (entries * lax.rsqrt(squares / full_width + EPSILON)[:, None]).astype(jnp.bfloat16)
    gathered = lax.all_gather(normed, "dp", axis=0, tiled=True)
    spread = gathered.astype(jnp.float32)
    hidden = (spread * norm_gain).astype(jnp.bfloat16)
    tangent = (spread * gain_dir).astype(jnp.bfloat16)
    logits = jnp.dot(hidden, head_weight, preferred_element_type=jnp.float32)
    tangent_logits = jnp.dot(hidden, head_dir, preferred_element_type=jnp.float32) + jnp.dot(
        tangent, head_weight, preferred_element_type=jnp.float32
    )
    logits, tangent_logits = (
        lax.psum_scatter(logits, "tensor", scatter_dimension=0, tiled=True),
        lax.psum_scatter(tangent_logits, "tensor", scatter_dimension=0, tiled=True),
    )
    share_rows = logits.shape[0]
    picked_ids = lax.dynamic_slice_in_dim(
        sampled, lax.axis_index("tensor") * share_rows, share_rows
    )
    vocab_dev = head_weight.shape[1]
    offset = (lax.axis_index("dp") * lax.axis_size("vocab") + lax.axis_index("vocab")) * vocab_dev
    is_picked = lax.broadcasted_iota(jnp.int32, logits.shape, 1) == (picked_ids - offset)[:, None]
    picked_part = jnp.sum(jnp.where(is_picked, tangent_logits, 0.0), axis=1)
    own_top = jnp.max(logits, axis=1)
    scaled_exp = jnp.exp(logits - own_top[:, None])
    own = jnp.stack(
        [own_top, jnp.sum(scaled_exp, axis=1), jnp.sum(scaled_exp * tangent_logits, axis=1), picked_part]
    )
    row_top, row_total, weighted, picked = merge_stats(own, ("dp", "vocab"))
    row_probs = scaled_exp * (jnp.exp(own_top - row_top) / row_total)[:, None]
    row_score = picked - weighted / row_total
    cotangent = (row_score[:, None] * (is_picked.astype(jnp.float32) - row_probs)).astype(
        jnp.bfloat16
    )
    full_cot = lax.all_gather(cotangent, "tensor", axis=0, tiled=True)
    product = lax.dot_general(
        gathered, full_cot, (((0,), (0,)), ((), ())), preferred_element_type=jnp.float32
    )
    fisher_head = norm_gain[:, None] * product
    fisher_gain = small_sum(
        jnp.sum(head_weight.astype(jnp.float32) * product, axis=1), ("dp", "vocab")
    )
    return (fisher_head, fisher_gain)


def solution(mesh):
    in_specs = (
        P("dp", "tensor"),
        P("tensor"),
        P("tensor"),
        P("tensor", ("dp", "vocab")),
        P("tensor", ("dp", "vocab")),
        P(),
    )
    out_specs = (P("tensor", ("dp", "vocab")), P("tensor"))
    return jax.shard_map(local, mesh=mesh, in_specs=in_specs, out_specs=out_specs, check_vma=False)
```

```python
import functools

import jax
import jax.numpy as jnp
from jax import lax
from jax.experimental import pallas as pl
from jax.experimental.pallas import tpu as pltpu
from jax.sharding import Mesh, PartitionSpec as P

EPSILON = 1e-06
F32 = jnp.float32
BF16 = jnp.bfloat16
I16 = jnp.int16
LANES = 128
TOP_CODE = 32000.0
MIB = 1024 * 1024
CHUNKS = (
    ((0, 0, 0), (0, 0, 1)),
    ((3, 0, 0), (3, 0, 1), (1, 0, 0), (1, 0, 1)),
    ((0, 1, 0), (0, 1, 1), (2, 0, 0), (2, 0, 1)),
    ((3, 1, 0), (3, 1, 1), (1, 1, 0), (1, 1, 1)),
    ((2, 1, 0), (2, 1, 1)),
)
BLOCKS = tuple(block for chunk in CHUNKS for block in chunk)


def whole(shape):
    return pl.BlockSpec(shape, lambda *_: (0,) * len(shape))


def front_kernel(*refs, pieces, steps, rows):
    x_refs = refs[:pieces]
    gain_ref, dir_ref, weight_ref, slope_ref, log_ref, code_ref, tan_ref, rows_ref = refs[pieces:]
    x = jnp.concatenate([r[...].astype(F32) for r in x_refs], axis=0)
    rows_ref[...] = x.astype(BF16)
    hidden = (x * gain_ref[...]).astype(BF16)
    tangent = (x * dir_ref[...]).astype(BF16)
    weight = weight_ref[...]
    log = jnp.dot(hidden, weight, preferred_element_type=F32)
    tan = jnp.dot(hidden, slope_ref[...], preferred_element_type=F32) + jnp.dot(
        tangent, weight, preferred_element_type=F32
    )
    step = pl.program_id(0)

    @pl.when(step == 0)
    def _():
        log_ref[...] = log
        tan_ref[...] = tan

    @pl.when(step > 0)
    def _():
        log_ref[...] += log
        tan_ref[...] += tan

    @pl.when(step == steps - 1)
    def _():
        value = log_ref[...]
        most = jnp.max(jnp.abs(value), axis=0, keepdims=True)
        scale = jnp.ceil(jnp.log2(jnp.maximum(most, 1e-30)) * 256.0)
        coded = jnp.round(value * (TOP_CODE * jnp.exp2(scale * (-1.0 / 256.0))))
        code_ref[:rows, :] = coded.astype(jnp.int32).astype(I16)
        code_ref[rows:, :] = jnp.broadcast_to(scale, (16, scale.shape[1])).astype(jnp.int32).astype(I16)


def front(pieces, gain, slope_gain, weight, slope, steps=2):
    rows = sum(p.shape[0] for p in pieces)
    width, cols = weight.shape
    part = width // steps
    return pl.pallas_call(
        functools.partial(front_kernel, pieces=len(pieces), steps=steps, rows=rows),
        grid=(steps,),
        in_specs=[pl.BlockSpec((p.shape[0], part), lambda k: (0, k)) for p in pieces]
        + [pl.BlockSpec((1, part), lambda k: (0, k))] * 2
        + [pl.BlockSpec((part, cols), lambda k: (k, 0))] * 2,
        out_specs=[
            whole((rows, cols)),
            whole((rows + 16, cols)),
            whole((rows, cols)),
            pl.BlockSpec((rows, part), lambda k: (0, k)),
        ],
        out_shape=[
            jax.ShapeDtypeStruct((rows, cols), F32),
            jax.ShapeDtypeStruct((rows + 16, cols), I16),
            jax.ShapeDtypeStruct((rows, cols), F32),
            jax.ShapeDtypeStruct((rows, width), BF16),
        ],
        compiler_params=pltpu.CompilerParams(vmem_limit_bytes=40 * MIB),
        cost_estimate=pl.CostEstimate(
            flops=6 * rows * width * cols,
            bytes_accessed=4 * width * cols + 4 * rows * width + 10 * rows * cols,
            transcendentals=0,
        ),
        name="front",
    )(*pieces, gain, slope_gain, weight, slope)


def column(rows_of_lanes, size):
    filled = jnp.concatenate(
        [rows_of_lanes, jnp.zeros((8 - rows_of_lanes.shape[0], LANES), F32)], axis=0
    )
    return filled.T[:size]


def expo_kernel(place_ref, log_ref, code_ref, tan_ref, ids_ref, e_ref, stats_ref, *, first, size, count):
    rows = size * count
    cols = log_ref.shape[1]
    scale = code_ref[rows:, :].astype(jnp.int32).astype(F32)[0:1]
    back = jnp.exp2(scale * (1.0 / 256.0)) * (1.0 / TOP_CODE)
    logits = log_ref[...] + code_ref[:rows, :].astype(jnp.int32).astype(F32) * back
    tan = tan_ref[...]
    top = jnp.max(logits, axis=1, keepdims=True)
    e = jnp.exp(logits - top)
    e_ref[...] = e
    total = jnp.sum(e, axis=1, keepdims=True)
    weighted = jnp.sum(e * tan, axis=1, keepdims=True)
    ids = jnp.concatenate(
        [column(ids_ref[pl.ds(place_ref[first + j], 1), :], size) for j in range(count)], axis=0
    )[:, 0:1]
    hit = lax.broadcasted_iota(jnp.int32, (rows, cols), 1).astype(F32) == ids
    picked = jnp.sum(jnp.where(hit, tan, 0.0), axis=1, keepdims=True)
    lane = lax.broadcasted_iota(jnp.int32, (rows, LANES), 1)
    stats = jnp.where(lane == 0, top, jnp.where(lane == 1, total, jnp.where(lane == 2, weighted, picked)))
    for j in range(count):
        block = jnp.concatenate(
            [stats[j * size : (j + 1) * size], jnp.zeros((LANES - size, LANES), F32)], axis=0
        ).T
        for i in range(4):
            stats_ref[i, j : j + 1, :] = block[i : i + 1, :]


def expo(place, log, code, tan, ids, first, size):
    rows, cols = log.shape
    count = rows // size
    return pl.pallas_call(
        functools.partial(expo_kernel, first=first, size=size, count=count),
        in_specs=[pl.BlockSpec(memory_space=pltpu.SMEM)] + [pl.BlockSpec(memory_space=pltpu.VMEM)] * 4,
        out_specs=[pl.BlockSpec(memory_space=pltpu.VMEM)] * 2,
        out_shape=[
            jax.ShapeDtypeStruct((rows, cols), F32),
            jax.ShapeDtypeStruct((4, count, LANES), F32),
        ],
        compiler_params=pltpu.CompilerParams(vmem_limit_bytes=40 * MIB),
        cost_estimate=pl.CostEstimate(
            flops=12 * rows * cols, bytes_accessed=14 * rows * cols, transcendentals=rows * cols
        ),
        name="expo",
    )(place, log, code, tan, ids)


def merge(parts):
    count = parts.shape[0]
    top = parts[0, 0]
    for s in range(1, count):
        top = jnp.maximum(top, parts[s, 0])
    total = jnp.zeros_like(top)
    weighted = jnp.zeros_like(top)
    picked = jnp.zeros_like(top)
    for s in range(count):
        factor = jnp.exp(parts[s, 0] - top)
        total += factor * parts[s, 1]
        weighted += factor * parts[s, 2]
        picked += parts[s, 3]
    return top, total, weighted, picked


def first_merge_kernel(place_ref, parts_ref, out_ref):
    merged = merge(parts_ref)
    for i in range(4):
        for b in range(len(BLOCKS)):
            out_ref[i, pl.ds(place_ref[b], 1), :] = merged[i][b : b + 1]


def last_merge_kernel(parts_ref, out_ref, *, repeats):
    top, total, weighted, picked = merge(parts_ref)
    total = total * (1.0 / repeats)
    score = picked - weighted / total
    out_ref[0] = top
    out_ref[1] = score
    out_ref[2] = score / total
    out_ref[3] = total


def small_kernel(kernel, name, shape, *args):
    specs = [
        pl.BlockSpec(memory_space=pltpu.SMEM if a.dtype == jnp.int32 else pltpu.VMEM) for a in args
    ]
    return pl.pallas_call(
        kernel,
        in_specs=specs,
        out_specs=pl.BlockSpec(memory_space=pltpu.VMEM),
        out_shape=jax.ShapeDtypeStruct(shape, F32),
        compiler_params=pltpu.CompilerParams(vmem_limit_bytes=16 * MIB),
        name=name,
    )(*args)


def product_kernel(*refs, chunks, size, pairs):
    place_ref, ids_ref, merged_ref = refs[:3]
    e_refs = refs[3 : 3 + chunks]
    stats_refs = refs[3 + chunks : 3 + 2 * chunks]
    x_refs = refs[3 + 2 * chunks : 3 + 3 * chunks]
    weight_ref, gain_ref, out_ref, part_ref, cot_ref = refs[3 + 3 * chunks :]

    @pl.when(pl.program_id(0) == 0)
    def _():
        base = 0
        for chunk in range(chunks):
            count = e_refs[chunk].shape[0] // size
            for j in range(0, count, 2):
                both = []
                for i in (j, j + 1):
                    spot = place_ref[base + i]
                    score = merged_ref[1, pl.ds(spot, 1), :]
                    own = stats_refs[chunk][0, i : i + 1, :]
                    coef = jnp.exp(own - merged_ref[0, pl.ds(spot, 1), :]) * merged_ref[2, pl.ds(spot, 1), :]
                    cols = column(
                        jnp.concatenate([coef, score, ids_ref[pl.ds(spot, 1), :]], axis=0), size
                    )
                    e = e_refs[chunk][i * size : (i + 1) * size, :]
                    hit = lax.broadcasted_iota(jnp.int32, e.shape, 1).astype(F32) == cols[:, 2:3]
                    both.append(jnp.where(hit, cols[:, 1:2], 0.0) - cols[:, 0:1] * e)
                start = (base + j) * size
                cot_ref[start : start + 2 * size, :] = jnp.concatenate(both, axis=0).astype(BF16)
            base += count

    x = jnp.concatenate([r[...] for r in x_refs], axis=0)
    product = lax.dot_general(x, cot_ref[...], (((0,), (0,)), ((), ())), preferred_element_type=F32)
    out_ref[...] = gain_ref[...] * product
    part = jnp.sum(weight_ref[...].astype(F32) * product, axis=1, keepdims=True)
    part_ref[...] = jnp.broadcast_to(part, (part.shape[0], LANES)).T[:8]


def finish(place, ids, merged, e, stats, x, weight, gain, size, block=512):
    width, cols = weight.shape
    rows = sum(a.shape[0] for a in x)
    chunks = len(x)
    return pl.pallas_call(
        functools.partial(product_kernel, chunks=chunks, size=size, pairs=rows // (2 * size)),
        grid=(width // block,),
        in_specs=[pl.BlockSpec(memory_space=pltpu.SMEM), whole(ids.shape), whole(merged.shape)]
        + [whole(a.shape) for a in e]
        + [whole(a.shape) for a in stats]
        + [pl.BlockSpec((a.shape[0], block), lambda i: (0, i)) for a in x]
        + [pl.BlockSpec((block, cols), lambda i: (i, 0)), pl.BlockSpec((block, 1), lambda i: (i, 0))],
        out_specs=[
            pl.BlockSpec((block, cols), lambda i: (i, 0)),
            pl.BlockSpec((8, block), lambda i: (0, i)),
        ],
        out_shape=[
            jax.ShapeDtypeStruct((width, cols), F32),
            jax.ShapeDtypeStruct((8, width), F32),
        ],
        scratch_shapes=[pltpu.VMEM((rows, cols), BF16)],
        compiler_params=pltpu.CompilerParams(vmem_limit_bytes=48 * MIB),
        cost_estimate=pl.CostEstimate(
            flops=2 * rows * width * cols,
            bytes_accessed=4 * rows * cols + 2 * rows * width + 6 * width * cols,
            transcendentals=0,
        ),
        name="product",
    )(place, ids, merged, *e, *stats, *x, weight, gain)


def everyone(x, axes):
    count = 1
    for axis in axes:
        count *= lax.axis_size(axis)
    copies = jnp.broadcast_to(x[None], (count,) + x.shape)
    return lax.all_to_all(copies, axes, 0, 0, tiled=True)


def shift(x, axes, by):
    count = 1
    for axis in axes:
        count *= lax.axis_size(axis)
    return lax.ppermute(x, axes, [(i, (i + by) % count) for i in range(count)])


def swap(x, axis):
    return lax.ppermute(x, (axis,), [(0, 1), (1, 0)])


def local(residual, norm_gain, gain_dir, head_weight, head_dir, sampled):
    size, width = residual.shape
    vocab_dev = head_weight.shape[1]
    x_at, y_at, c_at, z_at = (lax.axis_index(a) for a in ("x", "yh", "c", "z"))
    around = lax.axis_size("x")
    place = jnp.stack(
        [(((x_at + o) % around) * 2 + (y_at ^ h)) * 2 + (c_at ^ g) for o, h, g in BLOCKS]
    ).astype(jnp.int32)
    offset = (((x_at * 2 + y_at) * 2 + c_at) * lax.axis_size("z") + z_at) * vocab_dev
    ids = jnp.pad(
        (sampled - offset).astype(F32).reshape(len(BLOCKS), size), ((0, 0), (0, LANES - size))
    )
    gain_row, dir_row, gain_col = norm_gain[None], gain_dir[None], norm_gain[:, None]

    entries = residual.astype(F32)
    squares = lax.psum(jnp.sum(entries * entries, axis=1), "t")
    normed = (entries * lax.rsqrt(squares / (2 * width) + EPSILON)[:, None]).astype(BF16)

    half = (size // 2 + 8) // 16 * 16
    ring = ("yh", "t")
    up = shift(shift(normed[:half], ring, 1), ring, 1)
    down = shift(shift(normed[half:], ring, -1), ring, -1)
    across = jnp.concatenate([up, down], axis=0)
    got = {}
    for h, block in ((0, normed), (1, across)):
        before, after = shift(block, ("x",), 1), shift(block, ("x",), -1)
        far = [shift(before[:half], ("x",), 1), shift(after[half:], ("x",), -1)]
        for o, pieces in ((0, [block]), (3, [before]), (1, [after]), (2, far)):
            got[o, h, 0] = pieces
            got[o, h, 1] = [swap(p, "c") for p in pieces]

    logs, tans, xs, es, stats = [], [], [], [], []
    first = 0
    for chunk in CHUNKS:
        pieces = [p for b in chunk for p in got[b]]
        log, code, tan, rows = front(pieces, gain_row, dir_row, head_weight, head_dir)
        e, stat = expo(place, log, swap(code, "t"), tan, ids, first, size)
        xs.append(rows)
        es.append(e)
        stats.append(stat)
        first += len(chunk)
    own = jnp.concatenate(stats, axis=1)
    shape = own.shape
    near = small_kernel(first_merge_kernel, "first_merge", shape, place, everyone(own, ("z",)))
    merged = small_kernel(
        functools.partial(last_merge_kernel, repeats=2.0),
        "last_merge",
        shape,
        everyone(near, ("x", "yh", "c", "t")),
    )
    fisher_head, part = finish(place, ids, merged, es, stats, xs, head_weight, gain_col, size)
    part = jnp.sum(everyone(part[0], ("x", "yh", "c")), axis=0)
    fisher_gain = jnp.sum(everyone(part, ("z",)), axis=0)
    return (fisher_head, fisher_gain)


def solution(mesh):
    fine = Mesh(mesh.devices.reshape(4, 2, 2, 8, 2), ("x", "yh", "c", "z", "t"))
    dp, vocab = ("x", "yh", "c"), ("x", "yh", "c", "z")
    in_specs = (P(dp, "t"), P("t"), P("t"), P("t", vocab), P("t", vocab), P())
    out_specs = (P("t", vocab), P("t"))
    return jax.shard_map(local, mesh=fine, in_specs=in_specs, out_specs=out_specs, check_vma=False)
```

```python
import functools
import math

import jax
import jax.numpy as jnp
from jax import lax
from jax.experimental import pallas as pl
from jax.experimental.pallas import tpu as pltpu
from jax.sharding import Mesh, PartitionSpec as P

EPSILON = 1e-06
F32 = jnp.float32
BF16 = jnp.bfloat16
I16 = jnp.int16
LANES = 128
TOP_CODE = 32000.0
MIB = 1024 * 1024
CHUNKS = (
    ((0, 0, 0), (0, 0, 1)),
    ((1, 0, 0), (1, 0, 1), (2, 0, 0), (2, 0, 1)),
    ((0, 1, 0), (0, 1, 1), (3, 0, 0), (3, 0, 1)),
    ((1, 1, 0), (1, 1, 1), (2, 1, 0), (2, 1, 1)),
    ((3, 1, 0), (3, 1, 1)),
)
BLOCKS = tuple(block for chunk in CHUNKS for block in chunk)
FIRST = tuple(sum(len(chunk) for chunk in CHUNKS[:k]) for k in range(len(CHUNKS)))
VMEM_BYTES = 16 * MIB
ON_CHIP = pl.BlockSpec(memory_space=pltpu.VMEM)
SCALARS = pl.BlockSpec(memory_space=pltpu.SMEM)


def whole(shape):
    return pl.BlockSpec(shape, lambda *_: (0,) * len(shape))


def column(rows_of_lanes, size):
    filled = jnp.concatenate(
        [rows_of_lanes, jnp.zeros((8 - rows_of_lanes.shape[0], LANES), F32)], axis=0
    )
    return filled.T[:size]


def load_kernel(*refs, count):
    copies = [
        pltpu.make_async_copy(refs[i], refs[count + i], refs[2 * count].at[i]) for i in range(count)
    ]
    for copy in copies:
        copy.start()
    for copy in copies:
        copy.wait()


def load(*arrays):
    count = len(arrays)
    return pl.pallas_call(
        functools.partial(load_kernel, count=count),
        in_specs=[pl.BlockSpec(memory_space=pl.ANY)] * count,
        out_specs=[ON_CHIP] * count,
        out_shape=[pltpu.VMEM(a.shape, a.dtype) for a in arrays],
        scratch_shapes=[pltpu.SemaphoreType.DMA((count,))],
        compiler_params=pltpu.CompilerParams(vmem_limit_bytes=VMEM_BYTES),
        name="load",
    )(*arrays)


def front_kernel(*refs, pieces, rows):
    x_refs = refs[:pieces]
    gain_ref, dir_ref, weight_ref, slope_ref, log_ref, code_ref, tan_ref, rows_ref = refs[pieces:]
    x = jnp.concatenate([r[...].astype(F32) for r in x_refs], axis=0)
    rows_ref[...] = x.astype(BF16)
    hidden = (x * gain_ref[...]).astype(BF16)
    tangent = (x * dir_ref[...]).astype(BF16)
    weight = weight_ref[...]
    log = jnp.dot(hidden, weight, preferred_element_type=F32)
    log_ref[...] = log
    tan_ref[...] = jnp.dot(hidden, slope_ref[...], preferred_element_type=F32) + jnp.dot(
        tangent, weight, preferred_element_type=F32
    )
    most = jnp.max(jnp.abs(log), axis=0, keepdims=True)
    scale = jnp.ceil(jnp.log2(jnp.maximum(most, 1e-30)) * 256.0)
    coded = jnp.round(log * (TOP_CODE * jnp.exp2(scale * (-1.0 / 256.0))))
    code_ref[:rows, :] = coded.astype(jnp.int32).astype(I16)
    code_ref[rows:, :] = jnp.broadcast_to(scale, (16, scale.shape[1])).astype(jnp.int32).astype(I16)


def front(pieces, gain, slope_gain, weight, slope):
    rows = sum(p.shape[0] for p in pieces)
    width, cols = weight.shape
    return pl.pallas_call(
        functools.partial(front_kernel, pieces=len(pieces), rows=rows),
        in_specs=[ON_CHIP] * (len(pieces) + 4),
        out_specs=[ON_CHIP] * 4,
        out_shape=[
            pltpu.VMEM((rows, cols), F32),
            pltpu.VMEM((rows + 16, cols), I16),
            pltpu.VMEM((rows, cols), F32),
            pltpu.VMEM((rows, width), BF16),
        ],
        compiler_params=pltpu.CompilerParams(vmem_limit_bytes=VMEM_BYTES),
        cost_estimate=pl.CostEstimate(
            flops=6 * rows * width * cols, bytes_accessed=4 * rows * width, transcendentals=0
        ),
        name="front",
    )(*pieces, gain, slope_gain, weight, slope)


def expo_kernel(place_ref, log_ref, code_ref, tan_ref, ids_ref, e_ref, stats_ref, dense_ref, *, first, size, count):
    rows = size * count
    cols = log_ref.shape[1]
    scale = code_ref[rows:, :].astype(jnp.int32).astype(F32)[0:1]
    back = jnp.exp2(scale * (1.0 / 256.0)) * (1.0 / TOP_CODE)
    logits = log_ref[...] + code_ref[:rows, :].astype(jnp.int32).astype(F32) * back
    tan = tan_ref[...]
    top = jnp.max(logits, axis=1, keepdims=True)
    e = jnp.exp(logits - top)
    e_ref[...] = e
    total = jnp.sum(e, axis=1, keepdims=True)
    weighted = jnp.sum(e * tan, axis=1, keepdims=True)
    ids = jnp.concatenate(
        [column(ids_ref[pl.ds(place_ref[first + j], 1), :], size) for j in range(count)], axis=0
    )[:, 0:1]
    hit = lax.broadcasted_iota(jnp.int32, (rows, cols), 1).astype(F32) == ids
    picked = jnp.sum(jnp.where(hit, tan, 0.0), axis=1, keepdims=True)
    lane = lax.broadcasted_iota(jnp.int32, (rows, LANES), 1)
    stats = jnp.where(lane == 0, top, jnp.where(lane == 1, total, jnp.where(lane == 2, weighted, picked)))
    spare = jnp.zeros((-rows % LANES, LANES), F32)
    dense_ref[...] = jnp.concatenate([stats, spare], axis=0).T[:4, :rows]
    for j in range(count):
        block = jnp.concatenate(
            [stats[j * size : (j + 1) * size], jnp.zeros((LANES - size, LANES), F32)], axis=0
        ).T
        for i in range(4):
            stats_ref[i, j : j + 1, :] = block[i : i + 1, :]


def expo(place, log, code, tan, ids, first, size):
    rows, cols = log.shape
    count = rows // size
    return pl.pallas_call(
        functools.partial(expo_kernel, first=first, size=size, count=count),
        in_specs=[SCALARS] + [ON_CHIP] * 4,
        out_specs=[ON_CHIP] * 3,
        out_shape=[
            pltpu.VMEM(shape, F32) for shape in ((rows, cols), (4, count, LANES), (4, rows))
        ],
        compiler_params=pltpu.CompilerParams(vmem_limit_bytes=VMEM_BYTES),
        cost_estimate=pl.CostEstimate(
            flops=12 * rows * cols, bytes_accessed=2 * rows * cols, transcendentals=rows * cols
        ),
        name="expo",
    )(place, log, code, tan, ids)


def merge(parts):
    count = parts.shape[0]
    top = parts[0, 0:1]
    for s in range(1, count):
        top = jnp.maximum(top, parts[s, 0:1])
    total = jnp.zeros_like(top)
    weighted = jnp.zeros_like(top)
    picked = jnp.zeros_like(top)
    for s in range(count):
        factor = jnp.exp(parts[s, 0:1] - top)
        total += factor * parts[s, 1:2]
        weighted += factor * parts[s, 2:3]
        picked += parts[s, 3:4]
    return top, total, weighted, picked


def copies_kernel(*refs):
    joined = jnp.concatenate([r[...] for r in refs[:-1]], axis=1)
    for copy in range(refs[-1].shape[0]):
        refs[-1][copy] = joined


def first_merge_kernel(place_ref, parts_ref, out_ref, moved_ref, *, size):
    merged = jnp.concatenate(merge(parts_ref), axis=0)
    for b in range(len(BLOCKS)):
        moved_ref[place_ref[b], :, :size] = merged[:, b * size : (b + 1) * size]
    out_ref[...] = jnp.concatenate([moved_ref[b, :, :size] for b in range(len(BLOCKS))], axis=1)


def pair_merge_kernel(one_ref, other_ref, out_ref):
    merged = jnp.concatenate(merge(jnp.stack([one_ref[...], other_ref[...]])), axis=0)
    for copy in range(out_ref.shape[0]):
        out_ref[copy] = merged


def last_merge_kernel(parts_ref, out_ref, *, size, repeats):
    top, total, weighted, picked = merge(parts_ref)
    total = total * (1.0 / repeats)
    score = picked - weighted / total
    merged = jnp.concatenate([top, score, score / total, total], axis=0)
    for b in range(len(BLOCKS)):
        out_ref[b, :, :size] = merged[:, b * size : (b + 1) * size]


def small_kernel(kernel, name, shape, scratch, *args):
    return pl.pallas_call(
        kernel,
        in_specs=[SCALARS if a.dtype == jnp.int32 else ON_CHIP for a in args],
        out_specs=ON_CHIP,
        out_shape=pltpu.VMEM(shape, F32),
        scratch_shapes=[pltpu.VMEM(a, F32) for a in scratch],
        compiler_params=pltpu.CompilerParams(vmem_limit_bytes=VMEM_BYTES),
        name=name,
    )(*args)


def product_kernel(*refs, chunks, size, pairs):
    place_ref, ids_ref, merged_ref = refs[:3]
    e_refs = refs[3 : 3 + chunks]
    stats_refs = refs[3 + chunks : 3 + 2 * chunks]
    x_refs = refs[3 + 2 * chunks : 3 + 3 * chunks]
    weight_ref, gain_ref, out_ref, part_ref, cot_ref = refs[3 + 3 * chunks :]

    @pl.when(pl.program_id(0) == 0)
    def _():
        base = 0
        for chunk in range(chunks):
            count = e_refs[chunk].shape[0] // size
            for j in range(0, count, 2):
                both = []
                for i in (j, j + 1):
                    spot = place_ref[base + i]
                    found = merged_ref[spot]
                    score = found[1:2]
                    own = stats_refs[chunk][0, i : i + 1, :]
                    coef = jnp.exp(own - found[0:1]) * found[2:3]
                    cols = column(
                        jnp.concatenate([coef, score, ids_ref[pl.ds(spot, 1), :]], axis=0), size
                    )
                    e = e_refs[chunk][i * size : (i + 1) * size, :]
                    hit = lax.broadcasted_iota(jnp.int32, e.shape, 1).astype(F32) == cols[:, 2:3]
                    both.append(jnp.where(hit, cols[:, 1:2], 0.0) - cols[:, 0:1] * e)
                start = (base + j) * size
                cot_ref[start : start + 2 * size, :] = jnp.concatenate(both, axis=0).astype(BF16)
            base += count

    block = out_ref.shape[0]
    here = pl.ds(pl.multiple_of(pl.program_id(0) * block, block), block)
    x = jnp.concatenate([r[:, here] for r in x_refs], axis=0)
    product = lax.dot_general(x, cot_ref[...], (((0,), (0,)), ((), ())), preferred_element_type=F32)
    gain = jnp.broadcast_to(gain_ref[...], (8, gain_ref.shape[1])).T[:, 0:1]
    out_ref[...] = gain * product
    part = jnp.sum(weight_ref[here, :].astype(F32) * product, axis=1, keepdims=True)
    part_ref[...] = jnp.broadcast_to(part, (part.shape[0], LANES)).T[:1]


def finish(place, ids, merged, e, stats, x, weight, gain, size, block=512):
    width, cols = weight.shape
    rows = sum(a.shape[0] for a in x)
    chunks = len(x)
    return pl.pallas_call(
        functools.partial(product_kernel, chunks=chunks, size=size, pairs=rows // (2 * size)),
        grid=(width // block,),
        in_specs=[SCALARS]
        + [ON_CHIP] * (2 + 2 * chunks)
        + [ON_CHIP] * (chunks + 1)
        + [pl.BlockSpec((1, block), lambda i: (0, i))],
        out_specs=[
            pl.BlockSpec((block, cols), lambda i: (i, 0)),
            pl.BlockSpec((1, block), lambda i: (0, i)),
        ],
        out_shape=[
            jax.ShapeDtypeStruct((width, cols), F32),
            jax.ShapeDtypeStruct((1, width), F32),
        ],
        scratch_shapes=[pltpu.VMEM((rows, cols), BF16)],
        compiler_params=pltpu.CompilerParams(vmem_limit_bytes=VMEM_BYTES),
        cost_estimate=pl.CostEstimate(
            flops=2 * rows * width * cols,
            bytes_accessed=4 * width * cols,
            transcendentals=0,
        ),
        name="product",
    )(place, ids, merged, *e, *stats, *x, weight, gain)


def members(axes):
    return math.prod(lax.axis_size(axis) for axis in axes)


def everyone(x, axes):
    copies = jnp.broadcast_to(x[None], (members(axes),) + x.shape)
    return lax.all_to_all(copies, axes, 0, 0, tiled=True)


def along_x(x, by):
    count = lax.axis_size("x")
    pairs = [
        (2 * i + core, 2 * ((i + (by, -by)[core]) % count) + core) for i in range(count) for core in (0, 1)
    ]
    return lax.ppermute(x, ("x", "c"), pairs)


def along_y(x):
    def at(y, core):
        return (y // 2 * 2 + core) * 2 + y % 2

    count = lax.axis_size("yh") * lax.axis_size("t")
    pairs = [
        (at(y, core), at((y + (1, -1)[core]) % count, core)) for y in range(count) for core in (0, 1)
    ]
    return lax.ppermute(x, ("yh", "c", "t"), pairs)


def swap(x, axis):
    return lax.ppermute(x, (axis,), [(0, 1), (1, 0)])


def together(*values):
    return lax.optimization_barrier(values)


def local(residual, norm_gain, gain_dir, head_weight, head_dir, sampled):
    size, width = residual.shape
    vocab_dev = head_weight.shape[1]
    x_at, y_at, c_at, z_at = (lax.axis_index(a) for a in ("x", "yh", "c", "z"))
    around = lax.axis_size("x")
    place = []
    for way, h, g in BLOCKS:
        back = 1 - 2 * (c_at ^ g)
        x_of = x_at + (0, -back, back, 2)[way]
        place.append((((x_of + around) % around) * 2 + (y_at ^ h)) * 2 + (c_at ^ g))
    place = jnp.stack(place).astype(jnp.int32)
    offset = (((x_at * 2 + y_at) * 2 + c_at) * lax.axis_size("z") + z_at) * vocab_dev
    ids = jnp.pad(
        (sampled - offset).astype(F32).reshape(len(BLOCKS), size), ((0, 0), (0, LANES - size))
    )
    gain_row, dir_row = norm_gain[None], gain_dir[None]

    place, ids, residual, gain_row, dir_row = together(place, ids, residual, gain_row, dir_row)
    entries = residual.astype(F32)
    squares = lax.psum(jnp.sum(entries * entries, axis=1), "t")
    normed = (entries * lax.rsqrt(squares / (2 * width) + EPSILON)[:, None]).astype(BF16)

    weight, slope = load(head_weight, head_dir)

    def chunk_front(*pieces):
        return front(pieces, gain_row, dir_row, weight, slope)

    def chunk_expo(k, made, code):
        return expo(place, made[0], code, made[2], ids, FIRST[k], size)

    across = along_y(normed)
    one, two = along_x(normed, 1), along_x(normed, -1)
    own2 = swap(normed, "c")
    across, one, two, own2, weight, slope = together(across, one, two, own2, weight, slope)

    across = along_y(across)
    far = along_x(one, 1)
    one2, two2 = swap(one, "c"), swap(two, "c")
    made0 = chunk_front(normed, own2)
    code0 = swap(made0[1], "t")
    across, far, one, two, one2, two2, made0 = together(across, far, one, two, one2, two2, made0)

    y_one, y_two = along_x(across, 1), along_x(across, -1)
    across2, far2 = swap(across, "c"), swap(far, "c")
    made1 = chunk_front(one, one2, two, two2)
    code1 = swap(made1[1], "t")
    y_one, y_two, across, across2, far, far2, made1, code0 = together(
        y_one, y_two, across, across2, far, far2, made1, code0
    )

    y_far = along_x(y_one, 1)
    y_one2, y_two2 = swap(y_one, "c"), swap(y_two, "c")
    expo0 = chunk_expo(0, made0, code0)
    made2 = chunk_front(across, across2, far, far2)
    code2 = swap(made2[1], "t")
    y_far, y_one, y_two, y_one2, y_two2, made2, expo0, code1 = together(
        y_far, y_one, y_two, y_one2, y_two2, made2, expo0, code1
    )

    y_far2 = swap(y_far, "c")
    made3 = chunk_front(y_one, y_one2, y_two, y_two2)
    code3 = swap(made3[1], "t")
    y_far, y_far2, made3 = together(y_far, y_far2, made3)

    made4 = chunk_front(y_far, y_far2)
    code4 = swap(made4[1], "t")
    expo1 = chunk_expo(1, made1, code1)
    made4, expo1, code2 = together(made4, expo1, code2)

    expo2 = chunk_expo(2, made2, code2)
    expo2, code3 = together(expo2, code3)
    expo3 = chunk_expo(3, made3, code3)
    expo3, code4 = together(expo3, code4)
    expo4 = chunk_expo(4, made4, code4)
    xs = [m[3] for m in (made0, made1, made2, made3, made4)]
    es, stats, dense = zip(expo0, expo1, expo2, expo3, expo4)
    tokens = size * len(BLOCKS)
    own = small_kernel(copies_kernel, "copies", (lax.axis_size("z"), 4, tokens), [], *dense)
    rest = ("x", "yh", "t")
    spread = (len(BLOCKS), 4, LANES)
    along_z = small_kernel(
        functools.partial(first_merge_kernel, size=size),
        "first_merge",
        own.shape[1:],
        [spread],
        place,
        lax.all_to_all(own, "z", 0, 0, tiled=True),
    )
    on_chip = small_kernel(
        pair_merge_kernel, "pair_merge", (members(rest),) + own.shape[1:], [], along_z, swap(along_z, "c")
    )
    merged = small_kernel(
        functools.partial(last_merge_kernel, size=size, repeats=2.0),
        "last_merge",
        spread,
        [],
        lax.all_to_all(on_chip, rest, 0, 0, tiled=True),
    )
    fisher_head, part = finish(place, ids, merged, es, stats, xs, weight, gain_row, size)
    part = jnp.sum(everyone(part, ("x", "yh", "c")), axis=0)
    fisher_gain = jnp.sum(everyone(part, ("z",)), axis=(0, 1))
    return (fisher_head, fisher_gain)


def solution(mesh):
    fine = Mesh(mesh.devices.reshape(4, 2, 2, 8, 2), ("x", "yh", "c", "z", "t"))
    dp, vocab = ("x", "yh", "c"), ("x", "yh", "c", "z")
    in_specs = (P(dp, "t"), P("t"), P("t"), P("t", vocab), P("t", vocab), P())
    out_specs = (P("t", vocab), P("t"))
    return jax.shard_map(local, mesh=fine, in_specs=in_specs, out_specs=out_specs, check_vma=False)
```

```python
import functools
import math

import jax
import jax.numpy as jnp
from jax import lax
from jax.experimental import pallas as pl
from jax.experimental.pallas import tpu as pltpu
from jax.sharding import Mesh, PartitionSpec as P

EPSILON = 1e-06
F32 = jnp.float32
BF16 = jnp.bfloat16
I16 = jnp.int16
LANES = 128
TOP_CODE = 32000.0
MIB = 1024 * 1024
CHUNKS = (
    ((0, 0, 0), (0, 0, 1), (1, 0, 0), (2, 0, 0)),
    ((1, 0, 1), (2, 0, 1), (0, 1, 0), (3, 0, 0)),
    ((0, 1, 1), (3, 0, 1), (1, 1, 0), (2, 1, 0)),
    ((1, 1, 1), (2, 1, 1), (3, 1, 0), (3, 1, 1)),
)
BLOCKS = tuple(block for chunk in CHUNKS for block in chunk)
FIRST = tuple(sum(len(chunk) for chunk in CHUNKS[:k]) for k in range(len(CHUNKS)))
VMEM_BYTES = 16 * MIB
ON_CHIP = pl.BlockSpec(memory_space=pltpu.VMEM)
SCALARS = pl.BlockSpec(memory_space=pltpu.SMEM)


def whole(shape):
    return pl.BlockSpec(shape, lambda *_: (0,) * len(shape))


def column(rows_of_lanes, size):
    filled = jnp.concatenate(
        [rows_of_lanes, jnp.zeros((8 - rows_of_lanes.shape[0], LANES), F32)], axis=0
    )
    return filled.T[:size]


def load_kernel(*refs, count):
    copies = [
        pltpu.make_async_copy(refs[i], refs[count + i], refs[2 * count].at[i]) for i in range(count)
    ]
    for copy in copies:
        copy.start()
    for copy in copies:
        copy.wait()


def load(*arrays):
    count = len(arrays)
    return pl.pallas_call(
        functools.partial(load_kernel, count=count),
        in_specs=[pl.BlockSpec(memory_space=pl.ANY)] * count,
        out_specs=[ON_CHIP] * count,
        out_shape=[pltpu.VMEM(a.shape, a.dtype) for a in arrays],
        scratch_shapes=[pltpu.SemaphoreType.DMA((count,))],
        compiler_params=pltpu.CompilerParams(vmem_limit_bytes=VMEM_BYTES),
        name="load",
    )(*arrays)


def front_kernel(*refs, pieces, rows):
    x_refs = refs[:pieces]
    gain_ref, dir_ref, weight_ref, slope_ref, log_ref, code_ref, tan_ref, rows_ref = refs[pieces:]
    x = jnp.concatenate([r[...].astype(F32) for r in x_refs], axis=0)
    rows_ref[...] = x.astype(BF16)
    hidden = (x * gain_ref[...]).astype(BF16)
    tangent = (x * dir_ref[...]).astype(BF16)
    weight = weight_ref[...]
    log = jnp.dot(hidden, weight, preferred_element_type=F32)
    log_ref[...] = log
    tan_ref[...] = jnp.dot(hidden, slope_ref[...], preferred_element_type=F32) + jnp.dot(
        tangent, weight, preferred_element_type=F32
    )
    most = jnp.max(jnp.abs(log), axis=0, keepdims=True)
    scale = jnp.ceil(jnp.log2(jnp.maximum(most, 1e-30)) * 256.0)
    coded = jnp.round(log * (TOP_CODE * jnp.exp2(scale * (-1.0 / 256.0))))
    code_ref[:rows, :] = coded.astype(jnp.int32).astype(I16)
    code_ref[rows:, :] = jnp.broadcast_to(scale, (16, scale.shape[1])).astype(jnp.int32).astype(I16)


def front(pieces, gain, slope_gain, weight, slope):
    rows = sum(p.shape[0] for p in pieces)
    width, cols = weight.shape
    return pl.pallas_call(
        functools.partial(front_kernel, pieces=len(pieces), rows=rows),
        in_specs=[ON_CHIP] * (len(pieces) + 4),
        out_specs=[ON_CHIP] * 4,
        out_shape=[
            pltpu.VMEM((rows, cols), F32),
            pltpu.VMEM((rows + 16, cols), I16),
            pltpu.VMEM((rows, cols), F32),
            pltpu.VMEM((rows, width), BF16),
        ],
        compiler_params=pltpu.CompilerParams(vmem_limit_bytes=VMEM_BYTES),
        cost_estimate=pl.CostEstimate(
            flops=6 * rows * width * cols, bytes_accessed=4 * rows * width, transcendentals=0
        ),
        name="front",
    )(*pieces, gain, slope_gain, weight, slope)


def expo_kernel(place_ref, log_ref, code_ref, tan_ref, ids_ref, e_ref, stats_ref, dense_ref, *, first, size, count):
    rows = size * count
    cols = log_ref.shape[1]
    scale = code_ref[rows:, :].astype(jnp.int32).astype(F32)[0:1]
    back = jnp.exp2(scale * (1.0 / 256.0)) * (1.0 / TOP_CODE)
    logits = log_ref[...] + code_ref[:rows, :].astype(jnp.int32).astype(F32) * back
    tan = tan_ref[...]
    top = jnp.max(logits, axis=1, keepdims=True)
    e = jnp.exp(logits - top)
    e_ref[...] = e
    total = jnp.sum(e, axis=1, keepdims=True)
    weighted = jnp.sum(e * tan, axis=1, keepdims=True)
    ids = jnp.concatenate(
        [column(ids_ref[pl.ds(place_ref[first + j], 1), :], size) for j in range(count)], axis=0
    )[:, 0:1]
    hit = lax.broadcasted_iota(jnp.int32, (rows, cols), 1).astype(F32) == ids
    picked = jnp.sum(jnp.where(hit, tan, 0.0), axis=1, keepdims=True)
    lane = lax.broadcasted_iota(jnp.int32, (rows, LANES), 1)
    stats = jnp.where(lane == 0, top, jnp.where(lane == 1, total, jnp.where(lane == 2, weighted, picked)))
    spare = jnp.zeros((-rows % LANES, LANES), F32)
    dense_ref[...] = jnp.concatenate([stats, spare], axis=0).T[:4, :rows]
    for j in range(count):
        block = jnp.concatenate(
            [stats[j * size : (j + 1) * size], jnp.zeros((LANES - size, LANES), F32)], axis=0
        ).T
        for i in range(4):
            stats_ref[i, j : j + 1, :] = block[i : i + 1, :]


def expo(place, log, code, tan, ids, first, size):
    rows, cols = log.shape
    count = rows // size
    return pl.pallas_call(
        functools.partial(expo_kernel, first=first, size=size, count=count),
        in_specs=[SCALARS] + [ON_CHIP] * 4,
        out_specs=[ON_CHIP] * 3,
        out_shape=[
            pltpu.VMEM(shape, F32) for shape in ((rows, cols), (4, count, LANES), (4, rows))
        ],
        compiler_params=pltpu.CompilerParams(vmem_limit_bytes=VMEM_BYTES),
        cost_estimate=pl.CostEstimate(
            flops=12 * rows * cols, bytes_accessed=2 * rows * cols, transcendentals=rows * cols
        ),
        name="expo",
    )(place, log, code, tan, ids)


def merge(parts):
    count = parts.shape[0]
    top = parts[0, 0:1]
    for s in range(1, count):
        top = jnp.maximum(top, parts[s, 0:1])
    total = jnp.zeros_like(top)
    weighted = jnp.zeros_like(top)
    picked = jnp.zeros_like(top)
    for s in range(count):
        factor = jnp.exp(parts[s, 0:1] - top)
        total += factor * parts[s, 1:2]
        weighted += factor * parts[s, 2:3]
        picked += parts[s, 3:4]
    return top, total, weighted, picked


def copies_kernel(*refs):
    joined = jnp.concatenate([r[...] for r in refs[:-1]], axis=1)
    for copy in range(refs[-1].shape[0]):
        refs[-1][copy] = joined


def first_merge_kernel(place_ref, parts_ref, out_ref, moved_ref, *, size):
    merged = jnp.concatenate(merge(parts_ref), axis=0)
    for b in range(len(BLOCKS)):
        moved_ref[place_ref[b], :, :size] = merged[:, b * size : (b + 1) * size]
    out_ref[...] = jnp.concatenate([moved_ref[b, :, :size] for b in range(len(BLOCKS))], axis=1)


def pair_merge_kernel(one_ref, other_ref, out_ref):
    merged = jnp.concatenate(merge(jnp.stack([one_ref[...], other_ref[...]])), axis=0)
    for copy in range(out_ref.shape[0]):
        out_ref[copy] = merged


def last_merge_kernel(parts_ref, out_ref, *, size, repeats):
    top, total, weighted, picked = merge(parts_ref)
    total = total * (1.0 / repeats)
    score = picked - weighted / total
    merged = jnp.concatenate([top, score, score / total, total], axis=0)
    for b in range(len(BLOCKS)):
        out_ref[b, :, :size] = merged[:, b * size : (b + 1) * size]


def small_kernel(kernel, name, shape, scratch, *args):
    return pl.pallas_call(
        kernel,
        in_specs=[SCALARS if a.dtype == jnp.int32 else ON_CHIP for a in args],
        out_specs=ON_CHIP,
        out_shape=pltpu.VMEM(shape, F32),
        scratch_shapes=[pltpu.VMEM(a, F32) for a in scratch],
        compiler_params=pltpu.CompilerParams(vmem_limit_bytes=VMEM_BYTES),
        name=name,
    )(*args)


def product_kernel(*refs, chunks, size, pairs):
    place_ref, ids_ref, merged_ref = refs[:3]
    e_refs = refs[3 : 3 + chunks]
    stats_refs = refs[3 + chunks : 3 + 2 * chunks]
    x_refs = refs[3 + 2 * chunks : 3 + 3 * chunks]
    weight_ref, gain_ref, out_ref, part_ref, cot_ref = refs[3 + 3 * chunks :]

    @pl.when(pl.program_id(0) == 0)
    def _():
        base = 0
        for chunk in range(chunks):
            count = e_refs[chunk].shape[0] // size
            for j in range(0, count, 2):
                both = []
                for i in (j, j + 1):
                    spot = place_ref[base + i]
                    found = merged_ref[spot]
                    score = found[1:2]
                    own = stats_refs[chunk][0, i : i + 1, :]
                    coef = jnp.exp(own - found[0:1]) * found[2:3]
                    cols = column(
                        jnp.concatenate([coef, score, ids_ref[pl.ds(spot, 1), :]], axis=0), size
                    )
                    e = e_refs[chunk][i * size : (i + 1) * size, :]
                    hit = lax.broadcasted_iota(jnp.int32, e.shape, 1).astype(F32) == cols[:, 2:3]
                    both.append(jnp.where(hit, cols[:, 1:2], 0.0) - cols[:, 0:1] * e)
                start = (base + j) * size
                cot_ref[start : start + 2 * size, :] = jnp.concatenate(both, axis=0).astype(BF16)
            base += count

    block = out_ref.shape[0]
    here = pl.ds(pl.multiple_of(pl.program_id(0) * block, block), block)
    x = jnp.concatenate([r[:, here] for r in x_refs], axis=0)
    product = lax.dot_general(x, cot_ref[...], (((0,), (0,)), ((), ())), preferred_element_type=F32)
    gain = jnp.broadcast_to(gain_ref[...], (8, gain_ref.shape[1])).T[:, 0:1]
    out_ref[...] = gain * product
    part = jnp.sum(weight_ref[here, :].astype(F32) * product, axis=1, keepdims=True)
    part_ref[...] = jnp.broadcast_to(part, (part.shape[0], LANES)).T[:1]


def finish(place, ids, merged, e, stats, x, weight, gain, size, block=512):
    width, cols = weight.shape
    rows = sum(a.shape[0] for a in x)
    chunks = len(x)
    return pl.pallas_call(
        functools.partial(product_kernel, chunks=chunks, size=size, pairs=rows // (2 * size)),
        grid=(width // block,),
        in_specs=[SCALARS]
        + [ON_CHIP] * (2 + 2 * chunks)
        + [ON_CHIP] * (chunks + 1)
        + [pl.BlockSpec((1, block), lambda i: (0, i))],
        out_specs=[
            pl.BlockSpec((block, cols), lambda i: (i, 0)),
            pl.BlockSpec((1, block), lambda i: (0, i)),
        ],
        out_shape=[
            jax.ShapeDtypeStruct((width, cols), F32),
            jax.ShapeDtypeStruct((1, width), F32),
        ],
        scratch_shapes=[pltpu.VMEM((rows, cols), BF16)],
        compiler_params=pltpu.CompilerParams(vmem_limit_bytes=VMEM_BYTES),
        cost_estimate=pl.CostEstimate(
            flops=2 * rows * width * cols,
            bytes_accessed=4 * width * cols,
            transcendentals=0,
        ),
        name="product",
    )(place, ids, merged, *e, *stats, *x, weight, gain)


def members(axes):
    return math.prod(lax.axis_size(axis) for axis in axes)


def everyone(x, axes):
    copies = jnp.broadcast_to(x[None], (members(axes),) + x.shape)
    return lax.all_to_all(copies, axes, 0, 0, tiled=True)


def along_x(x, by):
    count = lax.axis_size("x")
    pairs = [
        (2 * i + core, 2 * ((i + (by, -by)[core]) % count) + core) for i in range(count) for core in (0, 1)
    ]
    return lax.ppermute(x, ("x", "c"), pairs)


def along_y(x):
    def at(y, core):
        return (y // 2 * 2 + core) * 2 + y % 2

    count = lax.axis_size("yh") * lax.axis_size("t")
    pairs = [
        (at(y, core), at((y + (1, -1)[core]) % count, core)) for y in range(count) for core in (0, 1)
    ]
    return lax.ppermute(x, ("yh", "c", "t"), pairs)


def swap(x, axis):
    return lax.ppermute(x, (axis,), [(0, 1), (1, 0)])


def together(*values):
    return lax.optimization_barrier(values)


def local(residual, norm_gain, gain_dir, head_weight, head_dir, sampled):
    size, width = residual.shape
    vocab_dev = head_weight.shape[1]
    x_at, y_at, c_at, z_at = (lax.axis_index(a) for a in ("x", "yh", "c", "z"))
    around = lax.axis_size("x")
    place = []
    for way, h, g in BLOCKS:
        back = 1 - 2 * (c_at ^ g)
        x_of = x_at + (0, -back, back, 2)[way]
        place.append((((x_of + around) % around) * 2 + (y_at ^ h)) * 2 + (c_at ^ g))
    place = jnp.stack(place).astype(jnp.int32)
    offset = (((x_at * 2 + y_at) * 2 + c_at) * lax.axis_size("z") + z_at) * vocab_dev
    ids = jnp.pad(
        (sampled - offset).astype(F32).reshape(len(BLOCKS), size), ((0, 0), (0, LANES - size))
    )
    gain_row, dir_row = norm_gain[None], gain_dir[None]

    place, ids, residual, gain_row, dir_row = together(place, ids, residual, gain_row, dir_row)
    entries = residual.astype(F32)
    squares = lax.psum(jnp.sum(entries * entries, axis=1), "t")
    normed = (entries * lax.rsqrt(squares / (2 * width) + EPSILON)[:, None]).astype(BF16)

    weight, slope = load(head_weight, head_dir)

    def chunk_front(*pieces):
        return front(pieces, gain_row, dir_row, weight, slope)

    def chunk_expo(k, made, code):
        return expo(place, made[0], code, made[2], ids, FIRST[k], size)

    across = along_y(normed)
    one, two = along_x(normed, 1), along_x(normed, -1)
    own2 = swap(normed, "c")
    across, one, two, own2, weight, slope = together(across, one, two, own2, weight, slope)

    across = along_y(across)
    far = along_x(one, 1)
    one2, two2 = swap(one, "c"), swap(two, "c")
    made0 = chunk_front(normed, own2, one, two)
    code0 = swap(made0[1], "t")
    across, far, one2, two2, made0 = together(across, far, one2, two2, made0)

    y_one, y_two = along_x(across, 1), along_x(across, -1)
    across2, far2 = swap(across, "c"), swap(far, "c")
    made1 = chunk_front(one2, two2, across, far)
    code1 = swap(made1[1], "t")
    y_one, y_two, across2, far2, made1, code0 = together(y_one, y_two, across2, far2, made1, code0)

    y_far = along_x(y_one, 1)
    y_one2, y_two2 = swap(y_one, "c"), swap(y_two, "c")
    expo0 = chunk_expo(0, made0, code0)
    made2 = chunk_front(across2, far2, y_one, y_two)
    code2 = swap(made2[1], "t")
    y_far, y_one2, y_two2, made2, expo0, code1 = together(y_far, y_one2, y_two2, made2, expo0, code1)

    y_far2 = swap(y_far, "c")
    expo1 = chunk_expo(1, made1, code1)
    y_far2, expo1 = together(y_far2, expo1)
    made3 = chunk_front(y_one2, y_two2, y_far, y_far2)
    code3 = swap(made3[1], "t")
    made3, code2 = together(made3, code2)
    expo2 = chunk_expo(2, made2, code2)
    expo2, code3 = together(expo2, code3)
    expo3 = chunk_expo(3, made3, code3)
    xs = [m[3] for m in (made0, made1, made2, made3)]
    es, stats, dense = zip(expo0, expo1, expo2, expo3)
    tokens = size * len(BLOCKS)
    own = small_kernel(copies_kernel, "copies", (lax.axis_size("z"), 4, tokens), [], *dense)
    rest = ("x", "yh", "t")
    spread = (len(BLOCKS), 4, LANES)
    along_z = small_kernel(
        functools.partial(first_merge_kernel, size=size),
        "first_merge",
        own.shape[1:],
        [spread],
        place,
        lax.all_to_all(own, "z", 0, 0, tiled=True),
    )
    on_chip = small_kernel(
        pair_merge_kernel, "pair_merge", (members(rest),) + own.shape[1:], [], along_z, swap(along_z, "c")
    )
    merged = small_kernel(
        functools.partial(last_merge_kernel, size=size, repeats=2.0),
        "last_merge",
        spread,
        [],
        lax.all_to_all(on_chip, rest, 0, 0, tiled=True),
    )
    fisher_head, part = finish(place, ids, merged, es, stats, xs, weight, gain_row, size)
    part = jnp.sum(everyone(part, ("x", "yh", "c")), axis=0)
    fisher_gain = jnp.sum(everyone(part, ("z",)), axis=(0, 1))
    return (fisher_head, fisher_gain)


def solution(mesh):
    fine = Mesh(mesh.devices.reshape(4, 2, 2, 8, 2), ("x", "yh", "c", "z", "t"))
    dp, vocab = ("x", "yh", "c"), ("x", "yh", "c", "z")
    in_specs = (P(dp, "t"), P("t"), P("t"), P("t", vocab), P("t", vocab), P())
    out_specs = (P("t", vocab), P("t"))
    return jax.shard_map(local, mesh=fine, in_specs=in_specs, out_specs=out_specs, check_vma=False)
```

```python
import functools
import math

import jax
import jax.numpy as jnp
from jax import lax
from jax.experimental import pallas as pl
from jax.experimental.pallas import tpu as pltpu
from jax.sharding import Mesh, PartitionSpec as P

EPSILON = 1e-06
F32 = jnp.float32
BF16 = jnp.bfloat16
I16 = jnp.int16
LANES = 128
TOP_CODE = 32000.0
MIB = 1024 * 1024
CHUNKS = (
    ((0, 0, 0), (0, 0, 1)),
    ((1, 0, 0), (2, 0, 0)),
    ((1, 0, 1), (2, 0, 1), (0, 1, 0), (3, 0, 0)),
    ((0, 1, 1), (3, 0, 1), (1, 1, 0), (2, 1, 0)),
    ((1, 1, 1), (2, 1, 1), (3, 1, 0), (3, 1, 1)),
)
BLOCKS = tuple(block for chunk in CHUNKS for block in chunk)
FIRST = tuple(sum(len(chunk) for chunk in CHUNKS[:k]) for k in range(len(CHUNKS)))
VMEM_BYTES = 16 * MIB
ON_CHIP = pl.BlockSpec(memory_space=pltpu.VMEM)
SCALARS = pl.BlockSpec(memory_space=pltpu.SMEM)


def whole(shape):
    return pl.BlockSpec(shape, lambda *_: (0,) * len(shape))


def column(rows_of_lanes, size):
    filled = jnp.concatenate(
        [rows_of_lanes, jnp.zeros((8 - rows_of_lanes.shape[0], LANES), F32)], axis=0
    )
    return filled.T[:size]


def load_kernel(*refs, count):
    copies = [
        pltpu.make_async_copy(refs[i], refs[count + i], refs[2 * count].at[i]) for i in range(count)
    ]
    for copy in copies:
        copy.start()
    for copy in copies:
        copy.wait()


def load(*arrays):
    count = len(arrays)
    return pl.pallas_call(
        functools.partial(load_kernel, count=count),
        in_specs=[pl.BlockSpec(memory_space=pl.ANY)] * count,
        out_specs=[ON_CHIP] * count,
        out_shape=[pltpu.VMEM(a.shape, a.dtype) for a in arrays],
        scratch_shapes=[pltpu.SemaphoreType.DMA((count,))],
        compiler_params=pltpu.CompilerParams(vmem_limit_bytes=VMEM_BYTES),
        name="load",
    )(*arrays)


def front_kernel(*refs, pieces, rows):
    x_refs = refs[:pieces]
    gain_ref, dir_ref, weight_ref, slope_ref, log_ref, code_ref, tan_ref, rows_ref = refs[pieces:]
    x = jnp.concatenate([r[...].astype(F32) for r in x_refs], axis=0)
    rows_ref[...] = x.astype(BF16)
    hidden = (x * gain_ref[...]).astype(BF16)
    tangent = (x * dir_ref[...]).astype(BF16)
    weight = weight_ref[...]
    log = jnp.dot(hidden, weight, preferred_element_type=F32)
    log_ref[...] = log
    tan_ref[...] = jnp.dot(hidden, slope_ref[...], preferred_element_type=F32) + jnp.dot(
        tangent, weight, preferred_element_type=F32
    )
    most = jnp.max(jnp.abs(log), axis=0, keepdims=True)
    scale = jnp.ceil(jnp.log2(jnp.maximum(most, 1e-30)) * 256.0)
    coded = jnp.round(log * (TOP_CODE * jnp.exp2(scale * (-1.0 / 256.0))))
    code_ref[:rows, :] = coded.astype(jnp.int32).astype(I16)
    code_ref[rows:, :] = jnp.broadcast_to(scale, (16, scale.shape[1])).astype(jnp.int32).astype(I16)


def front(pieces, gain, slope_gain, weight, slope):
    rows = sum(p.shape[0] for p in pieces)
    width, cols = weight.shape
    return pl.pallas_call(
        functools.partial(front_kernel, pieces=len(pieces), rows=rows),
        in_specs=[ON_CHIP] * (len(pieces) + 4),
        out_specs=[ON_CHIP] * 4,
        out_shape=[
            pltpu.VMEM((rows, cols), F32),
            pltpu.VMEM((rows + 16, cols), I16),
            pltpu.VMEM((rows, cols), F32),
            pltpu.VMEM((rows, width), BF16),
        ],
        compiler_params=pltpu.CompilerParams(vmem_limit_bytes=VMEM_BYTES),
        cost_estimate=pl.CostEstimate(
            flops=6 * rows * width * cols, bytes_accessed=4 * rows * width, transcendentals=0
        ),
        name="front",
    )(*pieces, gain, slope_gain, weight, slope)


def expo_kernel(place_ref, log_ref, code_ref, tan_ref, ids_ref, e_ref, stats_ref, dense_ref, *, first, size, count):
    rows = size * count
    cols = log_ref.shape[1]
    scale = code_ref[rows:, :].astype(jnp.int32).astype(F32)[0:1]
    back = jnp.exp2(scale * (1.0 / 256.0)) * (1.0 / TOP_CODE)
    logits = log_ref[...] + code_ref[:rows, :].astype(jnp.int32).astype(F32) * back
    tan = tan_ref[...]
    top = jnp.max(logits, axis=1, keepdims=True)
    e = jnp.exp(logits - top)
    e_ref[...] = e
    total = jnp.sum(e, axis=1, keepdims=True)
    weighted = jnp.sum(e * tan, axis=1, keepdims=True)
    ids = jnp.concatenate(
        [column(ids_ref[pl.ds(place_ref[first + j], 1), :], size) for j in range(count)], axis=0
    )[:, 0:1]
    hit = lax.broadcasted_iota(jnp.int32, (rows, cols), 1).astype(F32) == ids
    picked = jnp.sum(jnp.where(hit, tan, 0.0), axis=1, keepdims=True)
    lane = lax.broadcasted_iota(jnp.int32, (rows, LANES), 1)
    stats = jnp.where(lane == 0, top, jnp.where(lane == 1, total, jnp.where(lane == 2, weighted, picked)))
    spare = jnp.zeros((-rows % LANES, LANES), F32)
    dense_ref[...] = jnp.concatenate([stats, spare], axis=0).T[:4, :rows]
    for j in range(count):
        block = jnp.concatenate(
            [stats[j * size : (j + 1) * size], jnp.zeros((LANES - size, LANES), F32)], axis=0
        ).T
        for i in range(4):
            stats_ref[i, j : j + 1, :] = block[i : i + 1, :]


def expo(place, log, code, tan, ids, first, size):
    rows, cols = log.shape
    count = rows // size
    return pl.pallas_call(
        functools.partial(expo_kernel, first=first, size=size, count=count),
        in_specs=[SCALARS] + [ON_CHIP] * 4,
        out_specs=[ON_CHIP] * 3,
        out_shape=[
            pltpu.VMEM(shape, F32) for shape in ((rows, cols), (4, count, LANES), (4, rows))
        ],
        compiler_params=pltpu.CompilerParams(vmem_limit_bytes=VMEM_BYTES),
        cost_estimate=pl.CostEstimate(
            flops=12 * rows * cols, bytes_accessed=2 * rows * cols, transcendentals=rows * cols
        ),
        name="expo",
    )(place, log, code, tan, ids)


def merge(parts):
    count = parts.shape[0]
    top = parts[0, 0:1]
    for s in range(1, count):
        top = jnp.maximum(top, parts[s, 0:1])
    total = jnp.zeros_like(top)
    weighted = jnp.zeros_like(top)
    picked = jnp.zeros_like(top)
    for s in range(count):
        factor = jnp.exp(parts[s, 0:1] - top)
        total += factor * parts[s, 1:2]
        weighted += factor * parts[s, 2:3]
        picked += parts[s, 3:4]
    return top, total, weighted, picked


def copies_kernel(*refs):
    joined = jnp.concatenate([r[...] for r in refs[:-1]], axis=1)
    for copy in range(refs[-1].shape[0]):
        refs[-1][copy] = joined


def first_merge_kernel(place_ref, parts_ref, out_ref, moved_ref, *, size):
    merged = jnp.concatenate(merge(parts_ref), axis=0)
    for b in range(len(BLOCKS)):
        moved_ref[place_ref[b], :, :size] = merged[:, b * size : (b + 1) * size]
    out_ref[...] = jnp.concatenate([moved_ref[b, :, :size] for b in range(len(BLOCKS))], axis=1)


def pair_merge_kernel(one_ref, other_ref, out_ref):
    merged = jnp.concatenate(merge(jnp.stack([one_ref[...], other_ref[...]])), axis=0)
    for copy in range(out_ref.shape[0]):
        out_ref[copy] = merged


def last_merge_kernel(parts_ref, out_ref, *, size, repeats):
    top, total, weighted, picked = merge(parts_ref)
    total = total * (1.0 / repeats)
    score = picked - weighted / total
    merged = jnp.concatenate([top, score, score / total, total], axis=0)
    for b in range(len(BLOCKS)):
        out_ref[b, :, :size] = merged[:, b * size : (b + 1) * size]


def small_kernel(kernel, name, shape, scratch, *args):
    return pl.pallas_call(
        kernel,
        in_specs=[SCALARS if a.dtype == jnp.int32 else ON_CHIP for a in args],
        out_specs=ON_CHIP,
        out_shape=pltpu.VMEM(shape, F32),
        scratch_shapes=[pltpu.VMEM(a, F32) for a in scratch],
        compiler_params=pltpu.CompilerParams(vmem_limit_bytes=VMEM_BYTES),
        name=name,
    )(*args)


def product_kernel(*refs, chunks, size, pairs):
    place_ref, ids_ref, merged_ref = refs[:3]
    e_refs = refs[3 : 3 + chunks]
    stats_refs = refs[3 + chunks : 3 + 2 * chunks]
    x_refs = refs[3 + 2 * chunks : 3 + 3 * chunks]
    weight_ref, gain_ref, out_ref, part_ref, cot_ref = refs[3 + 3 * chunks :]

    @pl.when(pl.program_id(0) == 0)
    def _():
        base = 0
        for chunk in range(chunks):
            count = e_refs[chunk].shape[0] // size
            for j in range(0, count, 2):
                both = []
                for i in (j, j + 1):
                    spot = place_ref[base + i]
                    found = merged_ref[spot]
                    score = found[1:2]
                    own = stats_refs[chunk][0, i : i + 1, :]
                    coef = jnp.exp(own - found[0:1]) * found[2:3]
                    cols = column(
                        jnp.concatenate([coef, score, ids_ref[pl.ds(spot, 1), :]], axis=0), size
                    )
                    e = e_refs[chunk][i * size : (i + 1) * size, :]
                    hit = lax.broadcasted_iota(jnp.int32, e.shape, 1).astype(F32) == cols[:, 2:3]
                    both.append(jnp.where(hit, cols[:, 1:2], 0.0) - cols[:, 0:1] * e)
                start = (base + j) * size
                cot_ref[start : start + 2 * size, :] = jnp.concatenate(both, axis=0).astype(BF16)
            base += count

    block = out_ref.shape[0]
    here = pl.ds(pl.multiple_of(pl.program_id(0) * block, block), block)
    x = jnp.concatenate([r[:, here] for r in x_refs], axis=0)
    product = lax.dot_general(x, cot_ref[...], (((0,), (0,)), ((), ())), preferred_element_type=F32)
    gain = jnp.broadcast_to(gain_ref[...], (8, gain_ref.shape[1])).T[:, 0:1]
    out_ref[...] = gain * product
    part = jnp.sum(weight_ref[here, :].astype(F32) * product, axis=1, keepdims=True)
    part_ref[...] = jnp.broadcast_to(part, (part.shape[0], LANES)).T[:1]


def finish(place, ids, merged, e, stats, x, weight, gain, size, block=512):
    width, cols = weight.shape
    rows = sum(a.shape[0] for a in x)
    chunks = len(x)
    return pl.pallas_call(
        functools.partial(product_kernel, chunks=chunks, size=size, pairs=rows // (2 * size)),
        grid=(width // block,),
        in_specs=[SCALARS]
        + [ON_CHIP] * (2 + 2 * chunks)
        + [ON_CHIP] * (chunks + 1)
        + [pl.BlockSpec((1, block), lambda i: (0, i))],
        out_specs=[
            pl.BlockSpec((block, cols), lambda i: (i, 0)),
            pl.BlockSpec((1, block), lambda i: (0, i)),
        ],
        out_shape=[
            jax.ShapeDtypeStruct((width, cols), F32),
            jax.ShapeDtypeStruct((1, width), F32),
        ],
        scratch_shapes=[pltpu.VMEM((rows, cols), BF16)],
        compiler_params=pltpu.CompilerParams(vmem_limit_bytes=VMEM_BYTES),
        cost_estimate=pl.CostEstimate(
            flops=2 * rows * width * cols,
            bytes_accessed=4 * width * cols,
            transcendentals=0,
        ),
        name="product",
    )(place, ids, merged, *e, *stats, *x, weight, gain)


def members(axes):
    return math.prod(lax.axis_size(axis) for axis in axes)


def everyone(x, axes):
    copies = jnp.broadcast_to(x[None], (members(axes),) + x.shape)
    return lax.all_to_all(copies, axes, 0, 0, tiled=True)


def along_x(x, by):
    count = lax.axis_size("x")
    pairs = [
        (2 * i + core, 2 * ((i + (by, -by)[core]) % count) + core) for i in range(count) for core in (0, 1)
    ]
    return lax.ppermute(x, ("x", "c"), pairs)


def along_y(x):
    def at(y, core):
        return (y // 2 * 2 + core) * 2 + y % 2

    count = lax.axis_size("yh") * lax.axis_size("t")
    pairs = [
        (at(y, core), at((y + (1, -1)[core]) % count, core)) for y in range(count) for core in (0, 1)
    ]
    return lax.ppermute(x, ("yh", "c", "t"), pairs)


def swap(x, axis):
    return lax.ppermute(x, (axis,), [(0, 1), (1, 0)])


def together(*values):
    return lax.optimization_barrier(values)


def local(residual, norm_gain, gain_dir, head_weight, head_dir, sampled):
    size, width = residual.shape
    vocab_dev = head_weight.shape[1]
    x_at, y_at, c_at, z_at = (lax.axis_index(a) for a in ("x", "yh", "c", "z"))
    around = lax.axis_size("x")
    place = []
    for way, h, g in BLOCKS:
        back = 1 - 2 * (c_at ^ g)
        x_of = x_at + (0, -back, back, 2)[way]
        place.append((((x_of + around) % around) * 2 + (y_at ^ h)) * 2 + (c_at ^ g))
    place = jnp.stack(place).astype(jnp.int32)
    offset = (((x_at * 2 + y_at) * 2 + c_at) * lax.axis_size("z") + z_at) * vocab_dev
    ids = jnp.pad(
        (sampled - offset).astype(F32).reshape(len(BLOCKS), size), ((0, 0), (0, LANES - size))
    )
    gain_row, dir_row = norm_gain[None], gain_dir[None]

    place, ids, residual, gain_row, dir_row = together(place, ids, residual, gain_row, dir_row)
    entries = residual.astype(F32)
    squares = lax.psum(jnp.sum(entries * entries, axis=1), "t")
    normed = (entries * lax.rsqrt(squares / (2 * width) + EPSILON)[:, None]).astype(BF16)

    weight, slope = load(head_weight, head_dir)

    def chunk_front(*pieces):
        return front(pieces, gain_row, dir_row, weight, slope)

    def chunk_expo(k, made, code):
        return expo(place, made[0], code, made[2], ids, FIRST[k], size)

    across = along_y(normed)
    one, two = along_x(normed, 1), along_x(normed, -1)
    made0 = chunk_front(normed, swap(normed, "c"))
    code0 = swap(made0[1], "t")
    across, one, two, made0 = together(across, one, two, made0)

    across = along_y(across)
    far = along_x(one, 1)
    one2, two2 = swap(one, "c"), swap(two, "c")
    made1 = chunk_front(one, two)
    code1 = swap(made1[1], "t")
    across, far, one2, two2, made1, code0 = together(across, far, one2, two2, made1, code0)

    y_one, y_two = along_x(across, 1), along_x(across, -1)
    across2, far2 = swap(across, "c"), swap(far, "c")
    expo0 = chunk_expo(0, made0, code0)
    made2 = chunk_front(one2, two2, across, far)
    code2 = swap(made2[1], "t")
    y_one, y_two, across2, far2, made2, expo0, code1 = together(
        y_one, y_two, across2, far2, made2, expo0, code1
    )

    y_far = along_x(y_one, 1)
    y_one2, y_two2 = swap(y_one, "c"), swap(y_two, "c")
    expo1 = chunk_expo(1, made1, code1)
    made3 = chunk_front(across2, far2, y_one, y_two)
    code3 = swap(made3[1], "t")
    y_far, y_one2, y_two2, made3, expo1, code2 = together(y_far, y_one2, y_two2, made3, expo1, code2)

    y_far2 = swap(y_far, "c")
    expo2 = chunk_expo(2, made2, code2)
    y_far2, expo2 = together(y_far2, expo2)
    made4 = chunk_front(y_one2, y_two2, y_far, y_far2)
    code4 = swap(made4[1], "t")
    made4, code3 = together(made4, code3)
    expo3 = chunk_expo(3, made3, code3)
    expo3, code4 = together(expo3, code4)
    expo4 = chunk_expo(4, made4, code4)
    xs = [m[3] for m in (made0, made1, made2, made3, made4)]
    es, stats, dense = zip(expo0, expo1, expo2, expo3, expo4)
    tokens = size * len(BLOCKS)
    own = small_kernel(copies_kernel, "copies", (lax.axis_size("z"), 4, tokens), [], *dense)
    rest = ("x", "yh", "t")
    spread = (len(BLOCKS), 4, LANES)
    along_z = small_kernel(
        functools.partial(first_merge_kernel, size=size),
        "first_merge",
        own.shape[1:],
        [spread],
        place,
        lax.all_to_all(own, "z", 0, 0, tiled=True),
    )
    on_chip = small_kernel(
        pair_merge_kernel, "pair_merge", (members(rest),) + own.shape[1:], [], along_z, swap(along_z, "c")
    )
    merged = small_kernel(
        functools.partial(last_merge_kernel, size=size, repeats=2.0),
        "last_merge",
        spread,
        [],
        lax.all_to_all(on_chip, rest, 0, 0, tiled=True),
    )
    fisher_head, part = finish(place, ids, merged, es, stats, xs, weight, gain_row, size)
    part = jnp.sum(everyone(part, ("x", "yh", "c")), axis=0)
    fisher_gain = jnp.sum(everyone(part, ("z",)), axis=(0, 1))
    return (fisher_head, fisher_gain)


def solution(mesh):
    fine = Mesh(mesh.devices.reshape(4, 2, 2, 8, 2), ("x", "yh", "c", "z", "t"))
    dp, vocab = ("x", "yh", "c"), ("x", "yh", "c", "z")
    in_specs = (P(dp, "t"), P("t"), P("t"), P("t", vocab), P("t", vocab), P())
    out_specs = (P("t", vocab), P("t"))
    return jax.shard_map(local, mesh=fine, in_specs=in_specs, out_specs=out_specs, check_vma=False)
```

```python
import functools
import math

import jax
import jax.numpy as jnp
from jax import lax
from jax.experimental import pallas as pl
from jax.experimental.pallas import tpu as pltpu
from jax.sharding import Mesh, PartitionSpec as P

EPSILON = 1e-06
F32 = jnp.float32
BF16 = jnp.bfloat16
I16 = jnp.int16
LANES = 128
TOP_CODE = 32000.0
MIB = 1024 * 1024
CHUNKS = (
    ((0, 0, 0), (0, 0, 1)),
    ((1, 0, 0), (2, 0, 0)),
    ((1, 0, 1), (2, 0, 1), (0, 1, 0), (3, 0, 0)),
    ((0, 1, 1), (3, 0, 1), (1, 1, 0), (2, 1, 0)),
    ((1, 1, 1), (2, 1, 1), (3, 1, 0), (3, 1, 1)),
)
BLOCKS = tuple(block for chunk in CHUNKS for block in chunk)
FIRST = tuple(sum(len(chunk) for chunk in CHUNKS[:k]) for k in range(len(CHUNKS)))
VMEM_BYTES = 16 * MIB
ON_CHIP = pl.BlockSpec(memory_space=pltpu.VMEM)
SCALARS = pl.BlockSpec(memory_space=pltpu.SMEM)


def whole(shape):
    return pl.BlockSpec(shape, lambda *_: (0,) * len(shape))


def column(rows_of_lanes, size):
    filled = jnp.concatenate(
        [rows_of_lanes, jnp.zeros((8 - rows_of_lanes.shape[0], LANES), F32)], axis=0
    )
    return filled.T[:size]


def load_kernel(*refs, count):
    copies = [
        pltpu.make_async_copy(refs[i], refs[count + i], refs[2 * count].at[i]) for i in range(count)
    ]
    for copy in copies:
        copy.start()
    for copy in copies:
        copy.wait()


def load(*arrays):
    count = len(arrays)
    return pl.pallas_call(
        functools.partial(load_kernel, count=count),
        in_specs=[pl.BlockSpec(memory_space=pl.ANY)] * count,
        out_specs=[ON_CHIP] * count,
        out_shape=[pltpu.VMEM(a.shape, a.dtype) for a in arrays],
        scratch_shapes=[pltpu.SemaphoreType.DMA((count,))],
        compiler_params=pltpu.CompilerParams(vmem_limit_bytes=VMEM_BYTES),
        name="load",
    )(*arrays)


def front_kernel(*refs, pieces, rows):
    x_refs = refs[:pieces]
    gain_ref, dir_ref, weight_ref, slope_ref, log_ref, code_ref, tan_ref, rows_ref = refs[pieces:]
    x = jnp.concatenate([r[...].astype(F32) for r in x_refs], axis=0)
    rows_ref[...] = x.astype(BF16)
    hidden = (x * gain_ref[...]).astype(BF16)
    tangent = (x * dir_ref[...]).astype(BF16)
    weight = weight_ref[...]
    log = jnp.dot(hidden, weight, preferred_element_type=F32)
    log_ref[...] = log
    tan_ref[...] = jnp.dot(hidden, slope_ref[...], preferred_element_type=F32) + jnp.dot(
        tangent, weight, preferred_element_type=F32
    )
    most = jnp.max(jnp.abs(log), axis=0, keepdims=True)
    scale = jnp.ceil(jnp.log2(jnp.maximum(most, 1e-30)) * 256.0)
    coded = jnp.round(log * (TOP_CODE * jnp.exp2(scale * (-1.0 / 256.0))))
    code_ref[:rows, :] = coded.astype(jnp.int32).astype(I16)
    code_ref[rows:, :] = jnp.broadcast_to(scale, (16, scale.shape[1])).astype(jnp.int32).astype(I16)


def front(pieces, gain, slope_gain, weight, slope):
    rows = sum(p.shape[0] for p in pieces)
    width, cols = weight.shape
    return pl.pallas_call(
        functools.partial(front_kernel, pieces=len(pieces), rows=rows),
        in_specs=[ON_CHIP] * (len(pieces) + 4),
        out_specs=[ON_CHIP] * 4,
        out_shape=[
            pltpu.VMEM((rows, cols), F32),
            pltpu.VMEM((rows + 16, cols), I16),
            pltpu.VMEM((rows, cols), F32),
            pltpu.VMEM((rows, width), BF16),
        ],
        compiler_params=pltpu.CompilerParams(vmem_limit_bytes=VMEM_BYTES),
        cost_estimate=pl.CostEstimate(
            flops=6 * rows * width * cols, bytes_accessed=4 * rows * width, transcendentals=0
        ),
        name="front",
    )(*pieces, gain, slope_gain, weight, slope)


def expo_kernel(place_ref, log_ref, code_ref, tan_ref, ids_ref, e_ref, stats_ref, dense_ref, *, first, size, count):
    rows = size * count
    cols = log_ref.shape[1]
    scale = code_ref[rows:, :].astype(jnp.int32).astype(F32)[0:1]
    back = jnp.exp2(scale * (1.0 / 256.0)) * (1.0 / TOP_CODE)
    logits = log_ref[...] + code_ref[:rows, :].astype(jnp.int32).astype(F32) * back
    tan = tan_ref[...]
    top = jnp.max(logits, axis=1, keepdims=True)
    e = jnp.exp(logits - top)
    e_ref[...] = e
    total = jnp.sum(e, axis=1, keepdims=True)
    weighted = jnp.sum(e * tan, axis=1, keepdims=True)
    ids = jnp.concatenate(
        [column(ids_ref[pl.ds(place_ref[first + j], 1), :], size) for j in range(count)], axis=0
    )[:, 0:1]
    hit = lax.broadcasted_iota(jnp.int32, (rows, cols), 1).astype(F32) == ids
    picked = jnp.sum(jnp.where(hit, tan, 0.0), axis=1, keepdims=True)
    lane = lax.broadcasted_iota(jnp.int32, (rows, LANES), 1)
    stats = jnp.where(lane == 0, top, jnp.where(lane == 1, total, jnp.where(lane == 2, weighted, picked)))
    spare = jnp.zeros((-rows % LANES, LANES), F32)
    dense_ref[...] = jnp.concatenate([stats, spare], axis=0).T[:4, :rows]
    for j in range(count):
        block = jnp.concatenate(
            [stats[j * size : (j + 1) * size], jnp.zeros((LANES - size, LANES), F32)], axis=0
        ).T
        for i in range(4):
            stats_ref[i, j : j + 1, :] = block[i : i + 1, :]


def expo(place, log, code, tan, ids, first, size):
    rows, cols = log.shape
    count = rows // size
    return pl.pallas_call(
        functools.partial(expo_kernel, first=first, size=size, count=count),
        in_specs=[SCALARS] + [ON_CHIP] * 4,
        out_specs=[ON_CHIP] * 3,
        out_shape=[
            pltpu.VMEM(shape, F32) for shape in ((rows, cols), (4, count, LANES), (4, rows))
        ],
        compiler_params=pltpu.CompilerParams(vmem_limit_bytes=VMEM_BYTES),
        cost_estimate=pl.CostEstimate(
            flops=12 * rows * cols, bytes_accessed=2 * rows * cols, transcendentals=rows * cols
        ),
        name="expo",
    )(place, log, code, tan, ids)


def merge(parts):
    count = parts.shape[0]
    top = parts[0, 0:1]
    for s in range(1, count):
        top = jnp.maximum(top, parts[s, 0:1])
    total = jnp.zeros_like(top)
    weighted = jnp.zeros_like(top)
    picked = jnp.zeros_like(top)
    for s in range(count):
        factor = jnp.exp(parts[s, 0:1] - top)
        total += factor * parts[s, 1:2]
        weighted += factor * parts[s, 2:3]
        picked += parts[s, 3:4]
    return top, total, weighted, picked


def copies_kernel(*refs):
    joined = jnp.concatenate([r[...] for r in refs[:-1]], axis=1)
    for copy in range(refs[-1].shape[0]):
        refs[-1][copy] = joined


def first_merge_kernel(place_ref, parts_ref, out_ref, moved_ref, *, size):
    merged = jnp.concatenate(merge(parts_ref), axis=0)
    for b in range(len(BLOCKS)):
        moved_ref[place_ref[b], :, :size] = merged[:, b * size : (b + 1) * size]
    out_ref[...] = jnp.concatenate([moved_ref[b, :, :size] for b in range(len(BLOCKS))], axis=1)


def pair_merge_kernel(one_ref, other_ref, out_ref):
    merged = jnp.concatenate(merge(jnp.stack([one_ref[...], other_ref[...]])), axis=0)
    for copy in range(out_ref.shape[0]):
        out_ref[copy] = merged


def last_merge_kernel(parts_ref, out_ref, *, size, repeats):
    top, total, weighted, picked = merge(parts_ref)
    total = total * (1.0 / repeats)
    score = picked - weighted / total
    merged = jnp.concatenate([top, score, score / total, total], axis=0)
    for b in range(len(BLOCKS)):
        out_ref[b, :, :size] = merged[:, b * size : (b + 1) * size]


def small_kernel(kernel, name, shape, scratch, *args):
    return pl.pallas_call(
        kernel,
        in_specs=[SCALARS if a.dtype == jnp.int32 else ON_CHIP for a in args],
        out_specs=ON_CHIP,
        out_shape=pltpu.VMEM(shape, F32),
        scratch_shapes=[pltpu.VMEM(a, F32) for a in scratch],
        compiler_params=pltpu.CompilerParams(vmem_limit_bytes=VMEM_BYTES),
        name=name,
    )(*args)


def product_kernel(*refs, chunks, size, pairs):
    place_ref, ids_ref, merged_ref = refs[:3]
    e_refs = refs[3 : 3 + chunks]
    stats_refs = refs[3 + chunks : 3 + 2 * chunks]
    x_refs = refs[3 + 2 * chunks : 3 + 3 * chunks]
    weight_ref, gain_ref, out_ref, part_ref, cot_ref = refs[3 + 3 * chunks :]

    @pl.when(pl.program_id(0) == 0)
    def _():
        base = 0
        for chunk in range(chunks):
            count = e_refs[chunk].shape[0] // size
            for j in range(0, count, 2):
                both = []
                for i in (j, j + 1):
                    spot = place_ref[base + i]
                    found = merged_ref[spot]
                    score = found[1:2]
                    own = stats_refs[chunk][0, i : i + 1, :]
                    coef = jnp.exp(own - found[0:1]) * found[2:3]
                    cols = column(
                        jnp.concatenate([coef, score, ids_ref[pl.ds(spot, 1), :]], axis=0), size
                    )
                    e = e_refs[chunk][i * size : (i + 1) * size, :]
                    hit = lax.broadcasted_iota(jnp.int32, e.shape, 1).astype(F32) == cols[:, 2:3]
                    both.append(jnp.where(hit, cols[:, 1:2], 0.0) - cols[:, 0:1] * e)
                start = (base + j) * size
                cot_ref[start : start + 2 * size, :] = jnp.concatenate(both, axis=0).astype(BF16)
            base += count

    block = out_ref.shape[0]
    here = pl.ds(pl.multiple_of(pl.program_id(0) * block, block), block)
    x = jnp.concatenate([r[:, here] for r in x_refs], axis=0)
    product = lax.dot_general(x, cot_ref[...], (((0,), (0,)), ((), ())), preferred_element_type=F32)
    gain = jnp.broadcast_to(gain_ref[...], (8, gain_ref.shape[1])).T[:, 0:1]
    out_ref[...] = gain * product
    part = jnp.sum(weight_ref[here, :].astype(F32) * product, axis=1, keepdims=True)
    part_ref[...] = jnp.broadcast_to(part, (part.shape[0], LANES)).T[:1]


def finish(place, ids, merged, e, stats, x, weight, gain, size, block=512):
    width, cols = weight.shape
    rows = sum(a.shape[0] for a in x)
    chunks = len(x)
    return pl.pallas_call(
        functools.partial(product_kernel, chunks=chunks, size=size, pairs=rows // (2 * size)),
        grid=(width // block,),
        in_specs=[SCALARS]
        + [ON_CHIP] * (2 + 2 * chunks)
        + [ON_CHIP] * (chunks + 1)
        + [pl.BlockSpec((1, block), lambda i: (0, i))],
        out_specs=[
            pl.BlockSpec((block, cols), lambda i: (i, 0)),
            pl.BlockSpec((1, block), lambda i: (0, i)),
        ],
        out_shape=[
            jax.ShapeDtypeStruct((width, cols), F32),
            jax.ShapeDtypeStruct((1, width), F32),
        ],
        scratch_shapes=[pltpu.VMEM((rows, cols), BF16)],
        compiler_params=pltpu.CompilerParams(vmem_limit_bytes=VMEM_BYTES),
        cost_estimate=pl.CostEstimate(
            flops=2 * rows * width * cols,
            bytes_accessed=4 * width * cols,
            transcendentals=0,
        ),
        name="product",
    )(place, ids, merged, *e, *stats, *x, weight, gain)


def members(axes):
    return math.prod(lax.axis_size(axis) for axis in axes)


def everyone(x, axes):
    copies = jnp.broadcast_to(x[None], (members(axes),) + x.shape)
    return lax.all_to_all(copies, axes, 0, 0, tiled=True)


def along_x(x, by):
    count = lax.axis_size("x")
    pairs = [
        (2 * i + core, 2 * ((i + (by, -by)[core]) % count) + core) for i in range(count) for core in (0, 1)
    ]
    return lax.ppermute(x, ("x", "c"), pairs)


def along_y(x):
    def at(y, core):
        return (y // 2 * 2 + core) * 2 + y % 2

    count = lax.axis_size("yh") * lax.axis_size("t")
    pairs = [
        (at(y, core), at((y + (1, -1)[core]) % count, core)) for y in range(count) for core in (0, 1)
    ]
    return lax.ppermute(x, ("yh", "c", "t"), pairs)


def swap(x, axis):
    return lax.ppermute(x, (axis,), [(0, 1), (1, 0)])


def together(*values):
    return lax.optimization_barrier(values)


def local(residual, norm_gain, gain_dir, head_weight, head_dir, sampled):
    size, width = residual.shape
    vocab_dev = head_weight.shape[1]
    x_at, y_at, c_at, z_at = (lax.axis_index(a) for a in ("x", "yh", "c", "z"))
    around = lax.axis_size("x")
    place = []
    for way, h, g in BLOCKS:
        back = 1 - 2 * (c_at ^ g)
        x_of = x_at + (0, -back, back, 2)[way]
        place.append((((x_of + around) % around) * 2 + (y_at ^ h)) * 2 + (c_at ^ g))
    place = jnp.stack(place).astype(jnp.int32)
    offset = (((x_at * 2 + y_at) * 2 + c_at) * lax.axis_size("z") + z_at) * vocab_dev
    ids = jnp.pad(
        (sampled - offset).astype(F32).reshape(len(BLOCKS), size), ((0, 0), (0, LANES - size))
    )
    gain_row, dir_row = norm_gain[None], gain_dir[None]

    place, ids, residual, gain_row, dir_row = together(place, ids, residual, gain_row, dir_row)
    entries = residual.astype(F32)
    squares = lax.psum(jnp.sum(entries * entries, axis=1), "t")
    normed = (entries * lax.rsqrt(squares / (2 * width) + EPSILON)[:, None]).astype(BF16)

    weight, slope = load(head_weight, head_dir)

    def chunk_front(*pieces):
        return front(pieces, gain_row, dir_row, weight, slope)

    def chunk_expo(k, made, code):
        return expo(place, made[0], code, made[2], ids, FIRST[k], size)

    across = along_y(normed)
    one, two = along_x(normed, 1), along_x(normed, -1)
    made0 = chunk_front(normed, swap(normed, "c"))
    code0 = swap(made0[1], "t")
    across, one, two, made0 = together(across, one, two, made0)

    across = along_y(across)
    far = along_x(one, 1)
    one2, two2 = swap(one, "c"), swap(two, "c")
    made1 = chunk_front(one, two)
    code1 = swap(made1[1], "t")
    across, far, one2, two2, made1 = together(across, far, one2, two2, made1)

    y_one, y_two = along_x(across, 1), along_x(across, -1)
    made2 = chunk_front(one2, two2, across, far)
    code2 = swap(made2[1], "t")
    across, far, made2, code0, code1 = together(across, far, made2, code0, code1)
    across2, far2 = swap(across, "c"), swap(far, "c")
    expo0 = chunk_expo(0, made0, code0)
    y_one, y_two, across2, far2, expo0 = together(y_one, y_two, across2, far2, expo0)

    y_far = along_x(y_one, 1)
    made3 = chunk_front(across2, far2, y_one, y_two)
    code3 = swap(made3[1], "t")
    y_one, y_two, made3 = together(y_one, y_two, made3)
    y_one2, y_two2 = swap(y_one, "c"), swap(y_two, "c")
    expo1 = chunk_expo(1, made1, code1)
    y_far, y_one2, y_two2, expo1, code2 = together(y_far, y_one2, y_two2, expo1, code2)

    y_far2 = swap(y_far, "c")
    expo2 = chunk_expo(2, made2, code2)
    y_far2, expo2 = together(y_far2, expo2)
    made4 = chunk_front(y_one2, y_two2, y_far, y_far2)
    code4 = swap(made4[1], "t")
    made4, code3 = together(made4, code3)
    expo3 = chunk_expo(3, made3, code3)
    expo3, code4 = together(expo3, code4)
    expo4 = chunk_expo(4, made4, code4)
    xs = [m[3] for m in (made0, made1, made2, made3, made4)]
    es, stats, dense = zip(expo0, expo1, expo2, expo3, expo4)
    tokens = size * len(BLOCKS)
    own = small_kernel(copies_kernel, "copies", (lax.axis_size("z"), 4, tokens), [], *dense)
    rest = ("x", "yh", "t")
    spread = (len(BLOCKS), 4, LANES)
    along_z = small_kernel(
        functools.partial(first_merge_kernel, size=size),
        "first_merge",
        own.shape[1:],
        [spread],
        place,
        lax.all_to_all(own, "z", 0, 0, tiled=True),
    )
    on_chip = small_kernel(
        pair_merge_kernel, "pair_merge", (members(rest),) + own.shape[1:], [], along_z, swap(along_z, "c")
    )
    merged = small_kernel(
        functools.partial(last_merge_kernel, size=size, repeats=2.0),
        "last_merge",
        spread,
        [],
        lax.all_to_all(on_chip, rest, 0, 0, tiled=True),
    )
    fisher_head, part = finish(place, ids, merged, es, stats, xs, weight, gain_row, size)
    part = jnp.sum(everyone(part, ("x", "yh", "c")), axis=0)
    fisher_gain = jnp.sum(everyone(part, ("z",)), axis=(0, 1))
    return (fisher_head, fisher_gain)


def solution(mesh):
    fine = Mesh(mesh.devices.reshape(4, 2, 2, 8, 2), ("x", "yh", "c", "z", "t"))
    dp, vocab = ("x", "yh", "c"), ("x", "yh", "c", "z")
    in_specs = (P(dp, "t"), P("t"), P("t"), P("t", vocab), P("t", vocab), P())
    out_specs = (P("t", vocab), P("t"))
    return jax.shard_map(local, mesh=fine, in_specs=in_specs, out_specs=out_specs, check_vma=False)
```

```python
import functools
import math

import jax
import jax.numpy as jnp
from jax import lax
from jax.experimental import pallas as pl
from jax.experimental.pallas import tpu as pltpu
from jax.sharding import Mesh, PartitionSpec as P

EPSILON = 1e-06
F32 = jnp.float32
BF16 = jnp.bfloat16
I16 = jnp.int16
LANES = 128
TOP_CODE = 32000.0
MIB = 1024 * 1024
CHUNKS = (
    ((0, 0, 0), (0, 0, 1)),
    ((1, 0, 0), (2, 0, 0)),
    ((1, 0, 1), (2, 0, 1), (0, 1, 0), (3, 0, 0)),
    ((0, 1, 1), (3, 0, 1), (1, 1, 0), (2, 1, 0)),
    ((1, 1, 1), (2, 1, 1), (3, 1, 0), (3, 1, 1)),
)
BLOCKS = tuple(block for chunk in CHUNKS for block in chunk)
FIRST = tuple(sum(len(chunk) for chunk in CHUNKS[:k]) for k in range(len(CHUNKS)))
VMEM_BYTES = 16 * MIB
ON_CHIP = pl.BlockSpec(memory_space=pltpu.VMEM)
SCALARS = pl.BlockSpec(memory_space=pltpu.SMEM)


def whole(shape):
    return pl.BlockSpec(shape, lambda *_: (0,) * len(shape))


def column(rows_of_lanes, size):
    filled = jnp.concatenate(
        [rows_of_lanes, jnp.zeros((8 - rows_of_lanes.shape[0], LANES), F32)], axis=0
    )
    return filled.T[:size]


def load_kernel(place_ref, sampled_ref, *refs, count, size):
    sources, ids_ref, targets, sems = refs[:count], refs[count], refs[count + 1 : 2 * count + 1], refs[-1]
    copies = [pltpu.make_async_copy(f, t, sems.at[i]) for i, (f, t) in enumerate(zip(sources, targets))]
    for copy in copies:
        copy.start()
    ids = sampled_ref[...].astype(F32) - place_ref[len(BLOCKS)].astype(F32)
    ids_ref[...] = jnp.zeros_like(ids_ref)
    for b in range(len(BLOCKS)):
        ids_ref[b : b + 1, :size] = ids[:, b * size : (b + 1) * size]
    for copy in copies:
        copy.wait()


def load(place, sampled, *arrays):
    count = len(arrays)
    return pl.pallas_call(
        functools.partial(load_kernel, count=count, size=sampled.shape[1] // len(BLOCKS)),
        in_specs=[SCALARS, ON_CHIP] + [pl.BlockSpec(memory_space=pl.ANY)] * count,
        out_specs=[ON_CHIP] * (count + 1),
        out_shape=[pltpu.VMEM((len(BLOCKS), LANES), F32)]
        + [pltpu.VMEM(a.shape, a.dtype) for a in arrays],
        scratch_shapes=[pltpu.SemaphoreType.DMA((count,))],
        compiler_params=pltpu.CompilerParams(vmem_limit_bytes=VMEM_BYTES),
        name="load",
    )(place, sampled, *arrays)


def front_kernel(*refs, pieces, rows):
    x_refs = refs[:pieces]
    gain_ref, dir_ref, weight_ref, slope_ref, log_ref, code_ref, tan_ref, rows_ref = refs[pieces:]
    x = jnp.concatenate([r[...].astype(F32) for r in x_refs], axis=0)
    rows_ref[...] = x.astype(BF16)
    hidden = (x * gain_ref[...]).astype(BF16)
    tangent = (x * dir_ref[...]).astype(BF16)
    weight = weight_ref[...]
    log = jnp.dot(hidden, weight, preferred_element_type=F32)
    log_ref[...] = log
    tan_ref[...] = jnp.dot(hidden, slope_ref[...], preferred_element_type=F32) + jnp.dot(
        tangent, weight, preferred_element_type=F32
    )
    most = jnp.max(jnp.abs(log), axis=0, keepdims=True)
    scale = jnp.ceil(jnp.log2(jnp.maximum(most, 1e-30)) * 256.0)
    coded = jnp.round(log * (TOP_CODE * jnp.exp2(scale * (-1.0 / 256.0))))
    code_ref[:rows, :] = coded.astype(jnp.int32).astype(I16)
    code_ref[rows:, :] = jnp.broadcast_to(scale, (16, scale.shape[1])).astype(jnp.int32).astype(I16)


def front(pieces, gain, slope_gain, weight, slope):
    rows = sum(p.shape[0] for p in pieces)
    width, cols = weight.shape
    return pl.pallas_call(
        functools.partial(front_kernel, pieces=len(pieces), rows=rows),
        in_specs=[ON_CHIP] * (len(pieces) + 4),
        out_specs=[ON_CHIP] * 4,
        out_shape=[
            pltpu.VMEM((rows, cols), F32),
            pltpu.VMEM((rows + 16, cols), I16),
            pltpu.VMEM((rows, cols), F32),
            pltpu.VMEM((rows, width), BF16),
        ],
        compiler_params=pltpu.CompilerParams(vmem_limit_bytes=VMEM_BYTES),
        cost_estimate=pl.CostEstimate(
            flops=6 * rows * width * cols, bytes_accessed=4 * rows * width, transcendentals=0
        ),
        name="front",
    )(*pieces, gain, slope_gain, weight, slope)


def expo_kernel(place_ref, log_ref, code_ref, tan_ref, ids_ref, e_ref, stats_ref, dense_ref, *, first, size, count):
    rows = size * count
    cols = log_ref.shape[1]
    scale = code_ref[rows:, :].astype(jnp.int32).astype(F32)[0:1]
    back = jnp.exp2(scale * (1.0 / 256.0)) * (1.0 / TOP_CODE)
    logits = log_ref[...] + code_ref[:rows, :].astype(jnp.int32).astype(F32) * back
    tan = tan_ref[...]
    top = jnp.max(logits, axis=1, keepdims=True)
    e = jnp.exp(logits - top)
    e_ref[...] = e
    total = jnp.sum(e, axis=1, keepdims=True)
    weighted = jnp.sum(e * tan, axis=1, keepdims=True)
    ids = jnp.concatenate(
        [column(ids_ref[pl.ds(place_ref[first + j], 1), :], size) for j in range(count)], axis=0
    )[:, 0:1]
    hit = lax.broadcasted_iota(jnp.int32, (rows, cols), 1).astype(F32) == ids
    picked = jnp.sum(jnp.where(hit, tan, 0.0), axis=1, keepdims=True)
    lane = lax.broadcasted_iota(jnp.int32, (rows, LANES), 1)
    stats = jnp.where(lane == 0, top, jnp.where(lane == 1, total, jnp.where(lane == 2, weighted, picked)))
    spare = jnp.zeros((-rows % LANES, LANES), F32)
    dense_ref[...] = jnp.concatenate([stats, spare], axis=0).T[:4, :rows]
    for j in range(count):
        block = jnp.concatenate(
            [stats[j * size : (j + 1) * size], jnp.zeros((LANES - size, LANES), F32)], axis=0
        ).T
        for i in range(4):
            stats_ref[i, j : j + 1, :] = block[i : i + 1, :]


def expo(place, log, code, tan, ids, first, size):
    rows, cols = log.shape
    count = rows // size
    return pl.pallas_call(
        functools.partial(expo_kernel, first=first, size=size, count=count),
        in_specs=[SCALARS] + [ON_CHIP] * 4,
        out_specs=[ON_CHIP] * 3,
        out_shape=[
            pltpu.VMEM(shape, F32) for shape in ((rows, cols), (4, count, LANES), (4, rows))
        ],
        compiler_params=pltpu.CompilerParams(vmem_limit_bytes=VMEM_BYTES),
        cost_estimate=pl.CostEstimate(
            flops=12 * rows * cols, bytes_accessed=2 * rows * cols, transcendentals=rows * cols
        ),
        name="expo",
    )(place, log, code, tan, ids)


def merge(parts):
    count = parts.shape[0]
    top = parts[0, 0:1]
    for s in range(1, count):
        top = jnp.maximum(top, parts[s, 0:1])
    total = jnp.zeros_like(top)
    weighted = jnp.zeros_like(top)
    picked = jnp.zeros_like(top)
    for s in range(count):
        factor = jnp.exp(parts[s, 0:1] - top)
        total += factor * parts[s, 1:2]
        weighted += factor * parts[s, 2:3]
        picked += parts[s, 3:4]
    return top, total, weighted, picked


def copies_kernel(*refs):
    joined = jnp.concatenate([r[...] for r in refs[:-1]], axis=1)
    for copy in range(refs[-1].shape[0]):
        refs[-1][copy] = joined


def first_merge_kernel(place_ref, parts_ref, out_ref, moved_ref, *, size):
    merged = jnp.concatenate(merge(parts_ref), axis=0)
    for b in range(len(BLOCKS)):
        moved_ref[place_ref[b], :, :size] = merged[:, b * size : (b + 1) * size]
    out_ref[...] = jnp.concatenate([moved_ref[b, :, :size] for b in range(len(BLOCKS))], axis=1)


def pair_merge_kernel(one_ref, other_ref, out_ref):
    merged = jnp.concatenate(merge(jnp.stack([one_ref[...], other_ref[...]])), axis=0)
    for copy in range(out_ref.shape[0]):
        out_ref[copy] = merged


def last_merge_kernel(parts_ref, out_ref, *, size, repeats):
    top, total, weighted, picked = merge(parts_ref)
    total = total * (1.0 / repeats)
    score = picked - weighted / total
    merged = jnp.concatenate([top, score, score / total, total], axis=0)
    for b in range(len(BLOCKS)):
        out_ref[b, :, :size] = merged[:, b * size : (b + 1) * size]


def small_kernel(kernel, name, shape, scratch, *args):
    return pl.pallas_call(
        kernel,
        in_specs=[SCALARS if a.dtype == jnp.int32 else ON_CHIP for a in args],
        out_specs=ON_CHIP,
        out_shape=pltpu.VMEM(shape, F32),
        scratch_shapes=[pltpu.VMEM(a, F32) for a in scratch],
        compiler_params=pltpu.CompilerParams(vmem_limit_bytes=VMEM_BYTES),
        name=name,
    )(*args)


def product_kernel(*refs, chunks, size, pairs):
    place_ref, ids_ref, merged_ref = refs[:3]
    e_refs = refs[3 : 3 + chunks]
    stats_refs = refs[3 + chunks : 3 + 2 * chunks]
    x_refs = refs[3 + 2 * chunks : 3 + 3 * chunks]
    weight_ref, gain_ref, out_ref, part_ref, cot_ref = refs[3 + 3 * chunks :]

    @pl.when(pl.program_id(0) == 0)
    def _():
        base = 0
        for chunk in range(chunks):
            count = e_refs[chunk].shape[0] // size
            for j in range(0, count, 2):
                both = []
                for i in (j, j + 1):
                    spot = place_ref[base + i]
                    found = merged_ref[spot]
                    score = found[1:2]
                    own = stats_refs[chunk][0, i : i + 1, :]
                    coef = jnp.exp(own - found[0:1]) * found[2:3]
                    cols = column(
                        jnp.concatenate([coef, score, ids_ref[pl.ds(spot, 1), :]], axis=0), size
                    )
                    e = e_refs[chunk][i * size : (i + 1) * size, :]
                    hit = lax.broadcasted_iota(jnp.int32, e.shape, 1).astype(F32) == cols[:, 2:3]
                    both.append(jnp.where(hit, cols[:, 1:2], 0.0) - cols[:, 0:1] * e)
                start = (base + j) * size
                cot_ref[start : start + 2 * size, :] = jnp.concatenate(both, axis=0).astype(BF16)
            base += count

    block = out_ref.shape[0]
    here = pl.ds(pl.multiple_of(pl.program_id(0) * block, block), block)
    x = jnp.concatenate([r[:, here] for r in x_refs], axis=0)
    product = lax.dot_general(x, cot_ref[...], (((0,), (0,)), ((), ())), preferred_element_type=F32)
    gain = jnp.broadcast_to(gain_ref[...], (8, gain_ref.shape[1])).T[:, 0:1]
    out_ref[...] = gain * product
    part = jnp.sum(weight_ref[here, :].astype(F32) * product, axis=1, keepdims=True)
    part_ref[...] = jnp.broadcast_to(part, (part.shape[0], LANES)).T[:1]


def finish(place, ids, merged, e, stats, x, weight, gain, size, block=1024):
    width, cols = weight.shape
    rows = sum(a.shape[0] for a in x)
    chunks = len(x)
    return pl.pallas_call(
        functools.partial(product_kernel, chunks=chunks, size=size, pairs=rows // (2 * size)),
        grid=(width // block,),
        in_specs=[SCALARS]
        + [ON_CHIP] * (2 + 2 * chunks)
        + [ON_CHIP] * (chunks + 1)
        + [pl.BlockSpec((1, block), lambda i: (0, i))],
        out_specs=[
            pl.BlockSpec((block, cols), lambda i: (i, 0)),
            pl.BlockSpec((1, block), lambda i: (0, i)),
        ],
        out_shape=[
            jax.ShapeDtypeStruct((width, cols), F32),
            jax.ShapeDtypeStruct((1, width), F32),
        ],
        scratch_shapes=[pltpu.VMEM((rows, cols), BF16)],
        compiler_params=pltpu.CompilerParams(vmem_limit_bytes=VMEM_BYTES),
        cost_estimate=pl.CostEstimate(
            flops=2 * rows * width * cols,
            bytes_accessed=4 * width * cols,
            transcendentals=0,
        ),
        name="product",
    )(place, ids, merged, *e, *stats, *x, weight, gain)


def members(axes):
    return math.prod(lax.axis_size(axis) for axis in axes)


def everyone(x, axes):
    copies = jnp.broadcast_to(x[None], (members(axes),) + x.shape)
    return lax.all_to_all(copies, axes, 0, 0, tiled=True)


def along_x(x, by):
    count = lax.axis_size("x")
    pairs = [
        (2 * i + core, 2 * ((i + (by, -by)[core]) % count) + core) for i in range(count) for core in (0, 1)
    ]
    return lax.ppermute(x, ("x", "c"), pairs)


def along_y(x):
    def at(y, core):
        return (y // 2 * 2 + core) * 2 + y % 2

    count = lax.axis_size("yh") * lax.axis_size("t")
    pairs = [
        (at(y, core), at((y + (1, -1)[core]) % count, core)) for y in range(count) for core in (0, 1)
    ]
    return lax.ppermute(x, ("yh", "c", "t"), pairs)


def swap(x, axis):
    return lax.ppermute(x, (axis,), [(0, 1), (1, 0)])


def together(*values):
    return lax.optimization_barrier(values)


def local(residual, norm_gain, gain_dir, head_weight, head_dir, sampled):
    size, width = residual.shape
    vocab_dev = head_weight.shape[1]
    x_at, y_at, c_at, z_at = (lax.axis_index(a) for a in ("x", "yh", "c", "z"))
    around = lax.axis_size("x")
    place = []
    for way, h, g in BLOCKS:
        back = 1 - 2 * (c_at ^ g)
        x_of = x_at + (0, -back, back, 2)[way]
        place.append((((x_of + around) % around) * 2 + (y_at ^ h)) * 2 + (c_at ^ g))
    offset = (((x_at * 2 + y_at) * 2 + c_at) * lax.axis_size("z") + z_at) * vocab_dev
    place = jnp.stack(place + [offset]).astype(jnp.int32)
    sampled = sampled[None]
    gain_row, dir_row = norm_gain[None], gain_dir[None]

    place, sampled, residual, gain_row, dir_row = together(place, sampled, residual, gain_row, dir_row)
    entries = residual.astype(F32)
    squares = lax.psum(jnp.sum(entries * entries, axis=1), "t")
    normed = (entries * lax.rsqrt(squares / (2 * width) + EPSILON)[:, None]).astype(BF16)

    ids, weight, slope = load(place, sampled, head_weight, head_dir)

    def chunk_front(*pieces):
        return front(pieces, gain_row, dir_row, weight, slope)

    def chunk_expo(k, made, code):
        return expo(place, made[0], code, made[2], ids, FIRST[k], size)

    across = along_y(normed)
    one, two = along_x(normed, 1), along_x(normed, -1)
    made0 = chunk_front(normed, swap(normed, "c"))
    code0 = swap(made0[1], "t")
    across, one, two, made0 = together(across, one, two, made0)

    across = along_y(across)
    far = along_x(one, 1)
    one2, two2 = swap(one, "c"), swap(two, "c")
    made1 = chunk_front(one, two)
    code1 = swap(made1[1], "t")
    across, far, one2, two2, made1 = together(across, far, one2, two2, made1)

    y_one, y_two = along_x(across, 1), along_x(across, -1)
    made2 = chunk_front(one2, two2, across, far)
    code2 = swap(made2[1], "t")
    across, far, made2, code0, code1 = together(across, far, made2, code0, code1)
    across2, far2 = swap(across, "c"), swap(far, "c")
    expo0 = chunk_expo(0, made0, code0)
    y_one, y_two, across2, far2, expo0 = together(y_one, y_two, across2, far2, expo0)

    y_far = along_x(y_one, 1)
    made3 = chunk_front(across2, far2, y_one, y_two)
    code3 = swap(made3[1], "t")
    y_one, y_two, made3 = together(y_one, y_two, made3)
    y_one2, y_two2 = swap(y_one, "c"), swap(y_two, "c")
    expo1 = chunk_expo(1, made1, code1)
    y_far, y_one2, y_two2, expo1, code2 = together(y_far, y_one2, y_two2, expo1, code2)

    y_far2 = swap(y_far, "c")
    expo2 = chunk_expo(2, made2, code2)
    y_far2, expo2 = together(y_far2, expo2)
    made4 = chunk_front(y_one2, y_two2, y_far, y_far2)
    code4 = swap(made4[1], "t")
    made4, code3 = together(made4, code3)
    expo3 = chunk_expo(3, made3, code3)
    expo3, code4 = together(expo3, code4)
    expo4 = chunk_expo(4, made4, code4)
    xs = [m[3] for m in (made0, made1, made2, made3, made4)]
    es, stats, dense = zip(expo0, expo1, expo2, expo3, expo4)
    tokens = size * len(BLOCKS)
    own = small_kernel(copies_kernel, "copies", (lax.axis_size("z"), 4, tokens), [], *dense)
    rest = ("x", "yh", "t")
    spread = (len(BLOCKS), 4, LANES)
    along_z = small_kernel(
        functools.partial(first_merge_kernel, size=size),
        "first_merge",
        own.shape[1:],
        [spread],
        place,
        lax.all_to_all(own, "z", 0, 0, tiled=True),
    )
    on_chip = small_kernel(
        pair_merge_kernel, "pair_merge", (members(rest),) + own.shape[1:], [], along_z, swap(along_z, "c")
    )
    merged = small_kernel(
        functools.partial(last_merge_kernel, size=size, repeats=2.0),
        "last_merge",
        spread,
        [],
        lax.all_to_all(on_chip, rest, 0, 0, tiled=True),
    )
    fisher_head, part = finish(place, ids, merged, es, stats, xs, weight, gain_row, size)
    part = jnp.sum(everyone(part, ("x", "yh", "c")), axis=0)
    fisher_gain = jnp.sum(everyone(part, ("z",)), axis=(0, 1))
    return (fisher_head, fisher_gain)


def solution(mesh):
    fine = Mesh(mesh.devices.reshape(4, 2, 2, 8, 2), ("x", "yh", "c", "z", "t"))
    dp, vocab = ("x", "yh", "c"), ("x", "yh", "c", "z")
    in_specs = (P(dp, "t"), P("t"), P("t"), P("t", vocab), P("t", vocab), P())
    out_specs = (P("t", vocab), P("t"))
    return jax.shard_map(local, mesh=fine, in_specs=in_specs, out_specs=out_specs, check_vma=False)
```

```python
import functools
import math

import jax
import jax.numpy as jnp
from jax import lax
from jax.experimental import pallas as pl
from jax.experimental.pallas import tpu as pltpu
from jax.sharding import Mesh, PartitionSpec as P

EPSILON = 1e-06
F32 = jnp.float32
BF16 = jnp.bfloat16
I16 = jnp.int16
LANES = 128
TOP_CODE = 32000.0
MIB = 1024 * 1024
CHUNKS = (
    ((0, 0, 0), (0, 0, 1)),
    ((1, 0, 0), (2, 0, 0)),
    ((1, 0, 1), (2, 0, 1), (0, 1, 0), (3, 0, 0)),
    ((0, 1, 1), (3, 0, 1), (1, 1, 0), (2, 1, 0)),
    ((1, 1, 1), (2, 1, 1), (3, 1, 0), (3, 1, 1)),
)
BLOCKS = tuple(block for chunk in CHUNKS for block in chunk)
FIRST = tuple(sum(len(chunk) for chunk in CHUNKS[:k]) for k in range(len(CHUNKS)))
VMEM_BYTES = 16 * MIB
ON_CHIP = pl.BlockSpec(memory_space=pltpu.VMEM)
SCALARS = pl.BlockSpec(memory_space=pltpu.SMEM)


def whole(shape):
    return pl.BlockSpec(shape, lambda *_: (0,) * len(shape))


def column(rows_of_lanes, size):
    filled = jnp.concatenate(
        [rows_of_lanes, jnp.zeros((8 - rows_of_lanes.shape[0], LANES), F32)], axis=0
    )
    return filled.T[:size]


def load_kernel(*refs, count):
    copies = [
        pltpu.make_async_copy(refs[i], refs[count + i], refs[2 * count].at[i]) for i in range(count)
    ]
    for copy in copies:
        copy.start()
    for copy in copies:
        copy.wait()


def load(*arrays):
    count = len(arrays)
    return pl.pallas_call(
        functools.partial(load_kernel, count=count),
        in_specs=[pl.BlockSpec(memory_space=pl.ANY)] * count,
        out_specs=[ON_CHIP] * count,
        out_shape=[pltpu.VMEM(a.shape, a.dtype) for a in arrays],
        scratch_shapes=[pltpu.SemaphoreType.DMA((count,))],
        compiler_params=pltpu.CompilerParams(vmem_limit_bytes=VMEM_BYTES),
        name="load",
    )(*arrays)


def front_kernel(*refs, pieces, rows):
    x_refs = refs[:pieces]
    gain_ref, dir_ref, weight_ref, slope_ref, log_ref, code_ref, tan_ref, rows_ref = refs[pieces:]
    x = jnp.concatenate([r[...].astype(F32) for r in x_refs], axis=0)
    rows_ref[...] = x.astype(BF16)
    hidden = (x * gain_ref[...]).astype(BF16)
    tangent = (x * dir_ref[...]).astype(BF16)
    weight = weight_ref[...]
    log = jnp.dot(hidden, weight, preferred_element_type=F32)
    log_ref[...] = log
    tan_ref[...] = jnp.dot(hidden, slope_ref[...], preferred_element_type=F32) + jnp.dot(
        tangent, weight, preferred_element_type=F32
    )
    most = jnp.max(jnp.abs(log), axis=0, keepdims=True)
    scale = jnp.ceil(jnp.log2(jnp.maximum(most, 1e-30)) * 256.0)
    coded = jnp.round(log * (TOP_CODE * jnp.exp2(scale * (-1.0 / 256.0))))
    code_ref[:rows, :] = coded.astype(jnp.int32).astype(I16)
    code_ref[rows:, :] = jnp.broadcast_to(scale, (16, scale.shape[1])).astype(jnp.int32).astype(I16)


def front(pieces, gain, slope_gain, weight, slope):
    rows = sum(p.shape[0] for p in pieces)
    width, cols = weight.shape
    return pl.pallas_call(
        functools.partial(front_kernel, pieces=len(pieces), rows=rows),
        in_specs=[ON_CHIP] * (len(pieces) + 4),
        out_specs=[ON_CHIP] * 4,
        out_shape=[
            pltpu.VMEM((rows, cols), F32),
            pltpu.VMEM((rows + 16, cols), I16),
            pltpu.VMEM((rows, cols), F32),
            pltpu.VMEM((rows, width), BF16),
        ],
        compiler_params=pltpu.CompilerParams(vmem_limit_bytes=VMEM_BYTES),
        cost_estimate=pl.CostEstimate(
            flops=6 * rows * width * cols, bytes_accessed=4 * rows * width, transcendentals=0
        ),
        name="front",
    )(*pieces, gain, slope_gain, weight, slope)


def expo_kernel(place_ref, log_ref, code_ref, tan_ref, ids_ref, e_ref, stats_ref, dense_ref, *, first, size, count):
    rows = size * count
    cols = log_ref.shape[1]
    scale = code_ref[rows:, :].astype(jnp.int32).astype(F32)[0:1]
    back = jnp.exp2(scale * (1.0 / 256.0)) * (1.0 / TOP_CODE)
    logits = log_ref[...] + code_ref[:rows, :].astype(jnp.int32).astype(F32) * back
    tan = tan_ref[...]
    top = jnp.max(logits, axis=1, keepdims=True)
    e = jnp.exp(logits - top)
    e_ref[...] = e
    total = jnp.sum(e, axis=1, keepdims=True)
    weighted = jnp.sum(e * tan, axis=1, keepdims=True)
    ids = jnp.concatenate(
        [column(ids_ref[pl.ds(place_ref[first + j], 1), :], size) for j in range(count)], axis=0
    )[:, 0:1]
    hit = lax.broadcasted_iota(jnp.int32, (rows, cols), 1).astype(F32) == ids
    picked = jnp.sum(jnp.where(hit, tan, 0.0), axis=1, keepdims=True)
    lane = lax.broadcasted_iota(jnp.int32, (rows, LANES), 1)
    stats = jnp.where(lane == 0, top, jnp.where(lane == 1, total, jnp.where(lane == 2, weighted, picked)))
    spare = jnp.zeros((-rows % LANES, LANES), F32)
    dense_ref[...] = jnp.concatenate([stats, spare], axis=0).T[:4, :rows]
    for j in range(count):
        block = jnp.concatenate(
            [stats[j * size : (j + 1) * size], jnp.zeros((LANES - size, LANES), F32)], axis=0
        ).T
        for i in range(4):
            stats_ref[i, j : j + 1, :] = block[i : i + 1, :]


def expo(place, log, code, tan, ids, first, size):
    rows, cols = log.shape
    count = rows // size
    return pl.pallas_call(
        functools.partial(expo_kernel, first=first, size=size, count=count),
        in_specs=[SCALARS] + [ON_CHIP] * 4,
        out_specs=[ON_CHIP] * 3,
        out_shape=[
            pltpu.VMEM(shape, F32) for shape in ((rows, cols), (4, count, LANES), (4, rows))
        ],
        compiler_params=pltpu.CompilerParams(vmem_limit_bytes=VMEM_BYTES),
        cost_estimate=pl.CostEstimate(
            flops=12 * rows * cols, bytes_accessed=2 * rows * cols, transcendentals=rows * cols
        ),
        name="expo",
    )(place, log, code, tan, ids)


def merge(parts):
    count = parts.shape[0]
    top = parts[0, 0:1]
    for s in range(1, count):
        top = jnp.maximum(top, parts[s, 0:1])
    total = jnp.zeros_like(top)
    weighted = jnp.zeros_like(top)
    picked = jnp.zeros_like(top)
    for s in range(count):
        factor = jnp.exp(parts[s, 0:1] - top)
        total += factor * parts[s, 1:2]
        weighted += factor * parts[s, 2:3]
        picked += parts[s, 3:4]
    return top, total, weighted, picked


def copies_kernel(*refs):
    joined = jnp.concatenate([r[...] for r in refs[:-1]], axis=1)
    for copy in range(refs[-1].shape[0]):
        refs[-1][copy] = joined


def first_merge_kernel(place_ref, parts_ref, out_ref, moved_ref, *, size):
    merged = jnp.concatenate(merge(parts_ref), axis=0)
    for b in range(len(BLOCKS)):
        moved_ref[place_ref[b], :, :size] = merged[:, b * size : (b + 1) * size]
    out_ref[...] = jnp.concatenate([moved_ref[b, :, :size] for b in range(len(BLOCKS))], axis=1)


def pair_merge_kernel(one_ref, other_ref, out_ref):
    merged = jnp.concatenate(merge(jnp.stack([one_ref[...], other_ref[...]])), axis=0)
    for copy in range(out_ref.shape[0]):
        out_ref[copy] = merged


def last_merge_kernel(parts_ref, out_ref, *, size, repeats):
    top, total, weighted, picked = merge(parts_ref)
    total = total * (1.0 / repeats)
    score = picked - weighted / total
    merged = jnp.concatenate([top, score, score / total, total], axis=0)
    for b in range(len(BLOCKS)):
        out_ref[b, :, :size] = merged[:, b * size : (b + 1) * size]


def small_kernel(kernel, name, shape, scratch, *args):
    return pl.pallas_call(
        kernel,
        in_specs=[SCALARS if a.dtype == jnp.int32 else ON_CHIP for a in args],
        out_specs=ON_CHIP,
        out_shape=pltpu.VMEM(shape, F32),
        scratch_shapes=[pltpu.VMEM(a, F32) for a in scratch],
        compiler_params=pltpu.CompilerParams(vmem_limit_bytes=VMEM_BYTES),
        name=name,
    )(*args)


def product_kernel(*refs, chunks, size, pairs):
    place_ref, ids_ref, merged_ref = refs[:3]
    e_refs = refs[3 : 3 + chunks]
    stats_refs = refs[3 + chunks : 3 + 2 * chunks]
    x_refs = refs[3 + 2 * chunks : 3 + 3 * chunks]
    weight_ref, gain_ref, out_ref, part_ref, cot_ref = refs[3 + 3 * chunks :]

    @pl.when(pl.program_id(0) == 0)
    def _():
        base = 0
        for chunk in range(chunks):
            count = e_refs[chunk].shape[0] // size
            for j in range(0, count, 2):
                both = []
                for i in (j, j + 1):
                    spot = place_ref[base + i]
                    found = merged_ref[spot]
                    score = found[1:2]
                    own = stats_refs[chunk][0, i : i + 1, :]
                    coef = jnp.exp(own - found[0:1]) * found[2:3]
                    cols = column(
                        jnp.concatenate([coef, score, ids_ref[pl.ds(spot, 1), :]], axis=0), size
                    )
                    e = e_refs[chunk][i * size : (i + 1) * size, :]
                    hit = lax.broadcasted_iota(jnp.int32, e.shape, 1).astype(F32) == cols[:, 2:3]
                    both.append(jnp.where(hit, cols[:, 1:2], 0.0) - cols[:, 0:1] * e)
                start = (base + j) * size
                cot_ref[start : start + 2 * size, :] = jnp.concatenate(both, axis=0).astype(BF16)
            base += count

    block = out_ref.shape[0]
    here = pl.ds(pl.multiple_of(pl.program_id(0) * block, block), block)
    x = jnp.concatenate([r[:, here] for r in x_refs], axis=0)
    product = lax.dot_general(x, cot_ref[...], (((0,), (0,)), ((), ())), preferred_element_type=F32)
    gain = jnp.broadcast_to(gain_ref[...], (8, gain_ref.shape[1])).T[:, 0:1]
    out_ref[...] = gain * product
    part = jnp.sum(weight_ref[here, :].astype(F32) * product, axis=1, keepdims=True)
    part_ref[...] = jnp.broadcast_to(part, (part.shape[0], LANES)).T[:1]


def finish(place, ids, merged, e, stats, x, weight, gain, size, block=512):
    width, cols = weight.shape
    rows = sum(a.shape[0] for a in x)
    chunks = len(x)
    return pl.pallas_call(
        functools.partial(product_kernel, chunks=chunks, size=size, pairs=rows // (2 * size)),
        grid=(width // block,),
        in_specs=[SCALARS]
        + [ON_CHIP] * (2 + 2 * chunks)
        + [ON_CHIP] * (chunks + 1)
        + [pl.BlockSpec((1, block), lambda i: (0, i))],
        out_specs=[
            pl.BlockSpec((block, cols), lambda i: (i, 0)),
            pl.BlockSpec((1, block), lambda i: (0, i)),
        ],
        out_shape=[
            jax.ShapeDtypeStruct((width, cols), F32),
            jax.ShapeDtypeStruct((1, width), F32),
        ],
        scratch_shapes=[pltpu.VMEM((rows, cols), BF16)],
        compiler_params=pltpu.CompilerParams(vmem_limit_bytes=VMEM_BYTES),
        cost_estimate=pl.CostEstimate(
            flops=2 * rows * width * cols,
            bytes_accessed=4 * width * cols,
            transcendentals=0,
        ),
        name="product",
    )(place, ids, merged, *e, *stats, *x, weight, gain)


def members(axes):
    return math.prod(lax.axis_size(axis) for axis in axes)


def everyone(x, axes):
    copies = jnp.broadcast_to(x[None], (members(axes),) + x.shape)
    return lax.all_to_all(copies, axes, 0, 0, tiled=True)


def along_x(x, by):
    count = lax.axis_size("x")
    pairs = [
        (2 * i + core, 2 * ((i + (by, -by)[core]) % count) + core) for i in range(count) for core in (0, 1)
    ]
    return lax.ppermute(x, ("x", "c"), pairs)


def along_y(x):
    def at(y, core):
        return (y // 2 * 2 + core) * 2 + y % 2

    count = lax.axis_size("yh") * lax.axis_size("t")
    pairs = [
        (at(y, core), at((y + (1, -1)[core]) % count, core)) for y in range(count) for core in (0, 1)
    ]
    return lax.ppermute(x, ("yh", "c", "t"), pairs)


def swap(x, axis):
    return lax.ppermute(x, (axis,), [(0, 1), (1, 0)])


def together(*values):
    return lax.optimization_barrier(values)


def local(residual, norm_gain, gain_dir, head_weight, head_dir, sampled):
    size, width = residual.shape
    vocab_dev = head_weight.shape[1]
    x_at, y_at, c_at, z_at = (lax.axis_index(a) for a in ("x", "yh", "c", "z"))
    around = lax.axis_size("x")
    place = []
    for way, h, g in BLOCKS:
        back = 1 - 2 * (c_at ^ g)
        x_of = x_at + (0, -back, back, 2)[way]
        place.append((((x_of + around) % around) * 2 + (y_at ^ h)) * 2 + (c_at ^ g))
    place = jnp.stack(place).astype(jnp.int32)
    offset = (((x_at * 2 + y_at) * 2 + c_at) * lax.axis_size("z") + z_at) * vocab_dev
    ids = jnp.pad(
        (sampled - offset).astype(F32).reshape(len(BLOCKS), size), ((0, 0), (0, LANES - size))
    )
    gain_row, dir_row = norm_gain[None], gain_dir[None]

    place, ids, residual, gain_row, dir_row = together(place, ids, residual, gain_row, dir_row)
    entries = residual.astype(F32)
    squares = lax.psum(jnp.sum(entries * entries, axis=1), "t")
    normed = (entries * lax.rsqrt(squares / (2 * width) + EPSILON)[:, None]).astype(BF16)

    weight, slope = load(head_weight, head_dir)

    def chunk_front(*pieces):
        return front(pieces, gain_row, dir_row, weight, slope)

    def chunk_expo(k, made, code):
        return expo(place, made[0], code, made[2], ids, FIRST[k], size)

    across = along_y(normed)
    one, two = along_x(normed, 1), along_x(normed, -1)
    made0 = chunk_front(normed, swap(normed, "c"))
    code0 = swap(made0[1], "t")
    across, one, two, made0 = together(across, one, two, made0)

    across = along_y(across)
    far = along_x(one, 1)
    one2, two2 = swap(one, "c"), swap(two, "c")
    made1 = chunk_front(one, two)
    code1 = swap(made1[1], "t")
    across, far, one2, two2, made1 = together(across, far, one2, two2, made1)

    y_one, y_two = along_x(across, 1), along_x(across, -1)
    made2 = chunk_front(one2, two2, across, far)
    code2 = swap(made2[1], "t")
    across, far, made2, code0, code1 = together(across, far, made2, code0, code1)
    across2, far2 = swap(across, "c"), swap(far, "c")
    expo0 = chunk_expo(0, made0, code0)
    y_one, y_two, across2, far2, expo0 = together(y_one, y_two, across2, far2, expo0)

    y_far = along_x(y_one, 1)
    made3 = chunk_front(across2, far2, y_one, y_two)
    code3 = swap(made3[1], "t")
    y_one, y_two, made3 = together(y_one, y_two, made3)
    y_one2, y_two2 = swap(y_one, "c"), swap(y_two, "c")
    expo1 = chunk_expo(1, made1, code1)
    y_far, y_one2, y_two2, expo1, code2 = together(y_far, y_one2, y_two2, expo1, code2)
    made4 = chunk_front(y_one2, y_two2, y_far, swap(y_far, "c"))

    code4 = swap(made4[1], "t")
    expo2 = chunk_expo(2, made2, code2)
    made4, expo2, code3 = together(made4, expo2, code3)
    expo3 = chunk_expo(3, made3, code3)
    expo3, code4 = together(expo3, code4)
    expo4 = chunk_expo(4, made4, code4)
    xs = [m[3] for m in (made0, made1, made2, made3, made4)]
    es, stats, dense = zip(expo0, expo1, expo2, expo3, expo4)
    tokens = size * len(BLOCKS)
    own = small_kernel(copies_kernel, "copies", (lax.axis_size("z"), 4, tokens), [], *dense)
    rest = ("x", "yh", "t")
    spread = (len(BLOCKS), 4, LANES)
    along_z = small_kernel(
        functools.partial(first_merge_kernel, size=size),
        "first_merge",
        own.shape[1:],
        [spread],
        place,
        lax.all_to_all(own, "z", 0, 0, tiled=True),
    )
    on_chip = small_kernel(
        pair_merge_kernel, "pair_merge", (members(rest),) + own.shape[1:], [], along_z, swap(along_z, "c")
    )
    merged = small_kernel(
        functools.partial(last_merge_kernel, size=size, repeats=2.0),
        "last_merge",
        spread,
        [],
        lax.all_to_all(on_chip, rest, 0, 0, tiled=True),
    )
    fisher_head, part = finish(place, ids, merged, es, stats, xs, weight, gain_row, size)
    part = jnp.sum(everyone(part, ("x", "yh", "c")), axis=0)
    fisher_gain = jnp.sum(everyone(part, ("z",)), axis=(0, 1))
    return (fisher_head, fisher_gain)


def solution(mesh):
    fine = Mesh(mesh.devices.reshape(4, 2, 2, 8, 2), ("x", "yh", "c", "z", "t"))
    dp, vocab = ("x", "yh", "c"), ("x", "yh", "c", "z")
    in_specs = (P(dp, "t"), P("t"), P("t"), P("t", vocab), P("t", vocab), P())
    out_specs = (P("t", vocab), P("t"))
    return jax.shard_map(local, mesh=fine, in_specs=in_specs, out_specs=out_specs, check_vma=False)
```
